128 devices in a mesh: psg: 32 (over z, y_hi, x), cen: 4 (over y_lo, core).
Axes of the slice: x: 4, y: 4 (y_hi: 2, y_lo: 2; y = y_hi * 2 + y_lo), z: 4, core: 2. Of those that a mesh axis runs over, the one named last changes fastest.
Arguments:
- passages: bfloat16 [1024, 4096], P('psg'), may hold values from -8 to 8
- centroids: bfloat16 [65536, 4096], P(('psg', 'cen')), may hold values from -4 to 4
- dual_init: float32 [65536], P(('psg', 'cen')), may hold values from -8 to 8
Outputs:
- new_centroids: bfloat16 [65536, 4096], P(('psg', 'cen'))
- passage_duals: float32 [1024], P('psg')
- centroid_duals: float32 [65536], P(('psg', 'cen'))
The draws below stay inside these ranges and needn't reach their ends.
All inputs are finite; a program needn't handle non-finite values.
Results may differ from the reference program's by a relative error of at most 0.0047.
Values may be sent and summed in bfloat16 or wider, within the bound.
No kernel may reach another device: no remote copies, remote signals or barrier semaphores. Data moves between devices by JAX's collectives and lax.ppermute only.
A program may use at most 64 MiB of HBM per device.

```python
import math
import jax
import jax.numpy as jnp

D = 4096
CENTROIDS = 65536
ITERS = 3
PASSAGES = 1024


def centroid_table(key):
    table = jax.random.normal(key, (CENTROIDS, D), jnp.float32)
    return jnp.clip(table, -4.0, 4.0)


def draw_centroids(key, part):
    table = centroid_table(key)
    return table.astype(jnp.bfloat16)


def draw_passages(key, part):
    key = jax.random.fold_in(key, 3)
    values = jnp.clip(jax.random.normal(key, (PASSAGES, D), jnp.float32), -6.0, 6.0)
    return jnp.clip(values, -8.0, 8.0).astype(jnp.bfloat16)


def steps_of(rng, extent, shards, smallest, high):
    factor_of = 1.0
    for axis_at, blocks in shards:
        draws = jax.random.uniform(jax.random.fold_in(jax.random.fold_in(rng, 6), axis_at), (blocks,), jnp.float32, smallest / len(shards), high / len(shards))
        factor_of = factor_of * jnp.repeat(jnp.exp(draws), extent[axis_at] // blocks).reshape((-1,) + (1,) * (len(extent) - 1 - axis_at))
    return factor_of


def gaussian(own_key, shape, scale, limit, shards=(), held_as=jnp.bfloat16):
    entries = jax.random.normal(own_key, shape, jnp.float32) * scale
    if len(shards) > 0:
        entries = steps_of(own_key, shape, shards, -0.22, 0.18) * entries
    return jnp.clip(entries, min=-limit, max=limit).astype(held_as)


def setup_inputs(seed: int = 0) -> dict:
    splits = jax.random.split(jax.random.key(seed), 4)
    return {
        "passages": draw_passages(jax.random.fold_in(splits[3], 71), 0),
        "centroids": draw_centroids(jax.random.fold_in(splits[3], 71), 0),
        "dual_init": gaussian(splits[2], (CENTROIDS,), 2.0, 8.0, ((0, 128),), jnp.float32),
    }


def reference(passages, centroids, dual_init):
    factor = 4.0 / math.sqrt(D)
    logits = jnp.dot(passages, centroids.T, preferred_element_type=jnp.float32) * factor
    centroid_duals = dual_init
    passage_duals = jnp.zeros((PASSAGES,), jnp.float32)
    for number in range(ITERS):
        passage_duals = -math.log(PASSAGES) - jax.nn.logsumexp(logits + centroid_duals[None, :], axis=1)
        centroid_duals = -math.log(CENTROIDS) - jax.nn.logsumexp(logits + passage_duals[:, None], axis=0)
    weight = (CENTROIDS * jnp.exp(logits + passage_duals[:, None] + centroid_duals[None, :])).astype(jnp.bfloat16)
    new_centroids = jnp.dot(weight.T, passages, preferred_element_type=jnp.float32).astype(jnp.bfloat16)
    return (new_centroids, passage_duals, centroid_duals)
```

```python
import math

import jax
import jax.numpy as jnp
from jax import lax
from jax.sharding import PartitionSpec as P

CENTROIDS = 65536
PASSAGES = 1024
EVERY = ("psg", "cen")


def to_every(values):
    count = lax.axis_size(EVERY)
    return lax.all_to_all(jnp.broadcast_to(values[None], (count, *values.shape)), EVERY, 0, 0)


def total_over_devices(partial):
    return jnp.sum(to_every(partial.astype(jnp.bfloat16)).astype(jnp.float32), axis=0)


def body(passages, centroids, dual_init):
    factor = 4.0 / math.sqrt(passages.shape[1])
    local_rows = passages.shape[0]
    gathered = lax.all_gather(passages, "psg", axis=0, tiled=True)
    logits = factor * lax.dot_general(
        centroids, gathered, (((1,), (1,)), ((), ())), preferred_element_type=jnp.float32
    )

    shifted = logits + dual_init[:, None]
    top = jnp.max(shifted, axis=0)
    own = top + jnp.log(jnp.sum(jnp.exp(shifted - top[None, :]), axis=0))
    parts = to_every(own)
    top = jnp.max(parts, axis=0)
    passage_first = -math.log(PASSAGES) - (
        top + jnp.log(jnp.sum(jnp.exp(parts - top[None, :]), axis=0))
    )
    terms = logits + passage_first[None, :]
    top = jnp.max(terms, axis=1)
    total = jnp.sum(jnp.exp(terms - top[:, None]), axis=1)
    centroid_first = -math.log(CENTROIDS) - (top + jnp.log(total))

    kernel = jnp.exp(terms - top[:, None]) / total[:, None]
    ratio = CENTROIDS / PASSAGES
    row_scale = ratio / total_over_devices(jnp.sum(kernel, axis=0))
    col_scale = 1.0 / jnp.sum(kernel * row_scale[None, :], axis=1)
    row_scale = ratio / total_over_devices(jnp.sum(kernel * col_scale[:, None], axis=0))
    col_sum = jnp.sum(kernel * row_scale[None, :], axis=1)

    weight = (kernel * row_scale[None, :] / col_sum[:, None]).astype(jnp.bfloat16)
    new_centroids = lax.dot_general(
        weight, gathered, (((1,), (0,)), ((), ())), preferred_element_type=jnp.float32
    ).astype(jnp.bfloat16)
    passage_duals = passage_first + jnp.log(row_scale)
    own_duals = lax.dynamic_slice_in_dim(
        passage_duals, lax.axis_index("psg") * local_rows, local_rows
    )
    return (new_centroids, own_duals, centroid_first - jnp.log(col_sum))


def solution(mesh):
    in_specs = (P("psg", None), P(("psg", "cen"), None), P(("psg", "cen")))
    out_specs = (P(("psg", "cen"), None), P("psg"), P(("psg", "cen")))
    return jax.shard_map(body, mesh=mesh, in_specs=in_specs, out_specs=out_specs, check_vma=False)
```

```python
import math

import jax
import jax.numpy as jnp
from jax import lax
from jax.sharding import PartitionSpec as P

CENTROIDS = 65536
PASSAGES = 1024
EVERY = ("psg", "cen")
X, Z, HALVES, CORES = 4, 4, 2, 2


def coords(device):
    return (
        device // (HALVES * X * 4),
        device // (X * 4) % HALVES,
        device // 4 % X,
        device // 2 % 2,
        device % 2,
    )


def move(value, target):
    pairs = []
    for device in range(Z * HALVES * X * 4):
        there = target(*coords(device))
        if there is not None:
            z, h, x, l, c = there
            pairs.append((device, (((z % Z) * HALVES + h) * X + x % X) * 4 + l * 2 + c))
    return lax.ppermute(value, EVERY, pairs)


def along_first(value, step):
    return move(
        value,
        lambda z, h, x, l, c: (z, h, x + step, l, c) if c == 0 else (z + step, h, x, l, c),
    )


def along_second(value, step):
    return move(
        value,
        lambda z, h, x, l, c: (z + step, h, x, l, c) if c == 0 else (z, h, x + step, l, c),
    )


def to_sibling(value):
    return move(value, lambda z, h, x, l, c: (z, h, x, l, 1 - c))


def to_every(values):
    count = lax.axis_size(EVERY)
    return lax.all_to_all(jnp.broadcast_to(values[None], (count, *values.shape)), EVERY, 0, 0)


def total_over_devices(partial):
    return jnp.sum(to_every(partial.astype(jnp.bfloat16)).astype(jnp.float32), axis=0)


def turned(rows, places):
    return lax.dynamic_slice_in_dim(jnp.concatenate([rows, rows], 0), 4 - places, 4, 0)


def body(passages, centroids, dual_init):
    depth = passages.shape[1]
    local_rows = passages.shape[0]
    factor = 4.0 / math.sqrt(depth)
    z, h, x, _, c = coords(lax.axis_index(EVERY))
    first = jnp.where(c == 0, x, z)
    second = jnp.where(c == 0, z, x)

    other = move(passages, lambda z, h, x, l, c: (z, 1 - h, x, l, c) if h == c else None)
    mine = jnp.where(h == c, passages, other)
    ring = [mine, along_first(mine, -1), along_first(mine, 2), along_first(mine, 1)]
    ring = turned(jnp.stack(ring), first).reshape(4 * local_rows, depth)
    left, right = ring[:, : depth // 2], ring[:, depth // 2 :]
    left_before = along_second(left, 1)
    right_after = along_second(right, -1)
    right_before = along_second(right, 1)
    left_after = along_second(left, -1)
    left_across = along_second(left_before, 1)
    right_across = along_second(right_after, -1)
    own = [
        (left, right),
        (left_after, right_after),
        (left_across, right_across),
        (left_before, right_before),
    ]
    sibling = [(to_sibling(a), to_sibling(b)) for a, b in own]
    chunks = own + sibling

    def chunk_logits(pair):
        parts = [
            lax.dot_general(
                weights, part, (((1,), (1,)), ((), ())), preferred_element_type=jnp.float32
            )
            for weights, part in zip(
                (centroids[:, : depth // 2], centroids[:, depth // 2 :]), pair
            )
        ]
        return factor * (parts[0] + parts[1])

    logits = jnp.concatenate([chunk_logits(pair) for pair in chunks], axis=1)
    span = logits.shape[1] // 2

    def common(values):
        a, b = values.reshape(2, 4, span // 4)
        a, b = turned(a, second), turned(b, first)
        return jnp.where(c == 0, jnp.stack([a, b]), jnp.stack([b, a])).reshape(8, span // 4)

    def local(values):
        a, b = values.reshape(2, 4, span // 4)
        a, b = jnp.where(c == 0, a, b), jnp.where(c == 0, b, a)
        return jnp.stack([turned(a, (4 - second) % 4), turned(b, (4 - first) % 4)]).reshape(2 * span)

    shifted = logits + dual_init[:, None]
    top = jnp.max(shifted, axis=0)
    parts = to_every(common(top + jnp.log(jnp.sum(jnp.exp(shifted - top[None, :]), axis=0))))
    top = jnp.max(parts, axis=0)
    passage_first = -math.log(PASSAGES) - (
        top + jnp.log(jnp.sum(jnp.exp(parts - top[None]), axis=0))
    )
    terms = logits + local(passage_first)[None, :]
    top = jnp.max(terms, axis=1)
    total = jnp.sum(jnp.exp(terms - top[:, None]), axis=1)
    centroid_first = -math.log(CENTROIDS) - (top + jnp.log(total))

    kernel = jnp.exp(terms - top[:, None]) / total[:, None]
    ratio = CENTROIDS / PASSAGES
    row_scale = ratio / total_over_devices(common(jnp.sum(kernel, axis=0)))
    col_scale = 1.0 / jnp.sum(kernel * local(row_scale)[None, :], axis=1)
    row_scale = ratio / total_over_devices(common(jnp.sum(kernel * col_scale[:, None], axis=0)))
    scaled = kernel * local(row_scale)[None, :]
    col_sum = jnp.sum(scaled, axis=1)

    weight = (scaled / col_sum[:, None]).astype(jnp.bfloat16)
    new_centroids = jnp.concatenate(
        [
            lax.dot_general(
                weight,
                jnp.concatenate([pair[side] for pair in chunks], axis=0),
                (((1,), (0,)), ((), ())),
                preferred_element_type=jnp.float32,
            ).astype(jnp.bfloat16)
            for side in (0, 1)
        ],
        axis=1,
    )
    passage_duals = passage_first + jnp.log(row_scale)
    start = jnp.where(h == 0, z * X + x, (Z + x) * X + z) * local_rows
    own_duals = lax.dynamic_slice_in_dim(passage_duals.reshape(2 * span), start, local_rows)
    return (new_centroids, own_duals, centroid_first - jnp.log(col_sum))


def solution(mesh):
    in_specs = (P("psg", None), P(("psg", "cen"), None), P(("psg", "cen")))
    out_specs = (P(("psg", "cen"), None), P("psg"), P(("psg", "cen")))
    return jax.shard_map(body, mesh=mesh, in_specs=in_specs, out_specs=out_specs, check_vma=False)
```

```python
import math

import jax
import jax.numpy as jnp
from jax import lax
from jax.sharding import PartitionSpec as P

CENTROIDS = 65536
PASSAGES = 1024
EVERY = ("psg", "cen")
X, Z, HALVES, CORES = 4, 4, 2, 2


def coords(device):
    return (
        device // (HALVES * X * 4),
        device // (X * 4) % HALVES,
        device // 4 % X,
        device // 2 % 2,
        device % 2,
    )


def move(value, target):
    pairs = []
    for device in range(Z * HALVES * X * 4):
        there = target(*coords(device))
        if there is not None:
            z, h, x, l, c = there
            pairs.append((device, (((z % Z) * HALVES + h) * X + x % X) * 4 + l * 2 + c))
    return lax.ppermute(value, EVERY, pairs)


def along_second(value, step):
    return move(
        value,
        lambda z, h, x, l, c: (z + step, h, x, l, c) if c == 0 else (z, h, x + step, l, c),
    )


def to_sibling(value):
    return move(value, lambda z, h, x, l, c: (z, h, x, l, 1 - c))


def to_every(values):
    count = lax.axis_size(EVERY)
    return lax.all_to_all(jnp.broadcast_to(values[None], (count, *values.shape)), EVERY, 0, 0)


def total_over_devices(partial):
    return jnp.sum(to_every(partial.astype(jnp.bfloat16)).astype(jnp.float32), axis=0)


def turned(rows, places):
    return lax.dynamic_slice_in_dim(jnp.concatenate([rows, rows], 0), 4 - places, 4, 0)


def body(passages, centroids, dual_init):
    depth = passages.shape[1]
    local_rows = passages.shape[0]
    factor = 4.0 / math.sqrt(depth)
    z, h, x, _, c = coords(lax.axis_index(EVERY))
    first = jnp.where(c == 0, x, z)
    second = jnp.where(c == 0, z, x)

    def fetch(step):
        def target(z, h, x, l, c):
            stays = h == c
            if stays and step == 0:
                return None
            h, c = (h, c) if stays else (1 - h, 1 - c)
            return (z, h, x - step, l, c) if c == 0 else (z - step, h, x, l, c)

        return move(passages, target)

    ring = [jnp.where(h == c, passages, fetch(0)), fetch(1), fetch(2), fetch(3)]
    ring = turned(jnp.stack(ring), first).reshape(4 * local_rows, depth)
    own = [
        ring,
        along_second(ring, -1),
        along_second(ring, 2),
        along_second(ring, 1),
    ]
    chunks = own + [to_sibling(chunk) for chunk in own]

    def chunk_logits(chunk):
        return factor * lax.dot_general(
            centroids, chunk, (((1,), (1,)), ((), ())), preferred_element_type=jnp.float32
        )

    logits = jnp.concatenate([chunk_logits(chunk) for chunk in chunks], axis=1)
    span = logits.shape[1] // 2

    def common(values):
        a, b = values.reshape(2, 4, span // 4)
        a, b = turned(a, second), turned(b, first)
        return jnp.where(c == 0, jnp.stack([a, b]), jnp.stack([b, a])).reshape(8, span // 4)

    def local(values):
        a, b = values.reshape(2, 4, span // 4)
        a, b = jnp.where(c == 0, a, b), jnp.where(c == 0, b, a)
        return jnp.stack([turned(a, (4 - second) % 4), turned(b, (4 - first) % 4)]).reshape(2 * span)

    shifted = logits + dual_init[:, None]
    top = jnp.max(shifted, axis=0)
    parts = to_every(common(top + jnp.log(jnp.sum(jnp.exp(shifted - top[None, :]), axis=0))))
    top = jnp.max(parts, axis=0)
    passage_first = -math.log(PASSAGES) - (
        top + jnp.log(jnp.sum(jnp.exp(parts - top[None]), axis=0))
    )
    terms = logits + local(passage_first)[None, :]
    top = jnp.max(terms, axis=1)
    total = jnp.sum(jnp.exp(terms - top[:, None]), axis=1)
    centroid_first = -math.log(CENTROIDS) - (top + jnp.log(total))

    kernel = jnp.exp(terms - top[:, None]) / total[:, None]
    ratio = CENTROIDS / PASSAGES
    row_scale = ratio / total_over_devices(common(jnp.sum(kernel, axis=0)))
    col_scale = 1.0 / jnp.sum(kernel * local(row_scale)[None, :], axis=1)
    row_scale = ratio / total_over_devices(common(jnp.sum(kernel * col_scale[:, None], axis=0)))
    scaled = kernel * local(row_scale)[None, :]
    col_sum = jnp.sum(scaled, axis=1)

    weight = (scaled / col_sum[:, None]).astype(jnp.bfloat16)
    new_centroids = lax.dot_general(
        weight,
        jnp.concatenate(chunks, axis=0),
        (((1,), (0,)), ((), ())),
        preferred_element_type=jnp.float32,
    ).astype(jnp.bfloat16)
    passage_duals = passage_first + jnp.log(row_scale)
    start = jnp.where(h == 0, z * X + x, (Z + x) * X + z) * local_rows
    own_duals = lax.dynamic_slice_in_dim(passage_duals.reshape(2 * span), start, local_rows)
    return (new_centroids, own_duals, centroid_first - jnp.log(col_sum))


def solution(mesh):
    in_specs = (P("psg", None), P(("psg", "cen"), None), P(("psg", "cen")))
    out_specs = (P(("psg", "cen"), None), P("psg"), P(("psg", "cen")))
    return jax.shard_map(body, mesh=mesh, in_specs=in_specs, out_specs=out_specs, check_vma=False)
```

```python
import functools
import math

import jax
import jax.numpy as jnp
from jax import lax
from jax.experimental import pallas as pl
from jax.experimental.pallas import tpu as pltpu
from jax.sharding import PartitionSpec as P

CENTROIDS = 65536
PASSAGES = 1024
EVERY = ("psg", "cen")
X, Z, HALVES = 4, 4, 2
CHUNKS = 8
SLOTS = (0, 4, 2, 1, 3, 7, 6, 5)
LANES = 128
WIDTH = 1024


def coords(device):
    return (
        device // (HALVES * X * 4),
        device // (X * 4) % HALVES,
        device // 4 % X,
        device // 2 % 2,
        device % 2,
    )


def move(value, target):
    pairs = []
    for device in range(Z * HALVES * X * 4):
        there = target(*coords(device))
        if there is not None:
            z, h, x, l, c = there
            pairs.append((device, (((z % Z) * HALVES + h) * X + x % X) * 4 + l * 2 + c))
    return lax.ppermute(value, EVERY, pairs)


def along_second(value, step):
    return move(
        value,
        lambda z, h, x, l, c: (z + step, h, x, l, c) if c == 0 else (z, h, x + step, l, c),
    )


def to_sibling(value):
    return move(value, lambda z, h, x, l, c: (z, h, x, l, 1 - c))


def to_every(copies):
    return lax.all_to_all(copies, EVERY, 0, 0)


def turned(rows, places):
    return lax.dynamic_slice_in_dim(jnp.concatenate([rows, rows], 0), 4 - places, 4, 0)


def pair_kernel(factor, order_ref, duals_ref, centroids_ref, left_ref, right_ref, *refs):
    earlier, refs = refs[:-5], refs[-5:]
    logits_ref, out_ref, kept_ref, rows_ref, sem = refs
    span = left_ref.shape[0]
    total = lax.dot_general(
        centroids_ref[...],
        jnp.concatenate([left_ref[...], right_ref[...]], axis=0),
        (((1,), (1,)), ((), ())),
        preferred_element_type=jnp.float32,
    )
    for side in range(2):
        kept_ref[side] = factor * total[:, side * span : (side + 1) * span]
    copy_out = pltpu.make_async_copy(kept_ref, logits_ref, sem)
    copy_out.start()
    first = 2 * len(earlier)
    for side in range(2):
        shifted = kept_ref[side] + duals_ref[...]
        top = jnp.max(shifted, axis=0, keepdims=True)
        logsum = top + jnp.log(jnp.sum(jnp.exp(shifted - top), axis=0, keepdims=True))
        if earlier:
            rows_ref[pl.ds(order_ref[first + side], 1), :] = logsum
        else:
            out_ref[side : side + 1, :] = logsum
    if earlier:
        for pair, ref in enumerate(earlier):
            for side in range(2):
                rows_ref[pl.ds(order_ref[2 * pair + side], 1), :] = ref[side : side + 1, :]
        send_sums(rows_ref, out_ref)
    copy_out.wait()


def pair_logits(factor, order, duals, centroids, left, right, earlier=()):
    count, depth = centroids.shape
    span = left.shape[0]
    devices = lax.axis_size(EVERY)
    f32 = jnp.float32
    if earlier:
        out_spec = pl.BlockSpec((devices, CHUNKS, span), lambda: (0, 0, 0))
        out = jax.ShapeDtypeStruct((devices, CHUNKS, span), f32)
    else:
        out_spec, out = VMEM, jax.ShapeDtypeStruct((2, span), f32)
    return pl.pallas_call(
        functools.partial(pair_kernel, factor),
        in_specs=[SMEM] + [VMEM] * (4 + len(earlier)),
        out_specs=[ANY, out_spec],
        out_shape=[jax.ShapeDtypeStruct((2, count, span), f32), out],
        scratch_shapes=[
            pltpu.VMEM((2, count, span), f32),
            pltpu.VMEM((CHUNKS, span), f32),
            pltpu.SemaphoreType.DMA,
        ],
        cost_estimate=pl.CostEstimate(flops=1, bytes_accessed=1, transcendentals=0),
        compiler_params=LIMIT,
    )(order, duals, centroids, left, right, *earlier)


def send_sums(sums_ref, out_ref):
    out_ref[...] = jnp.broadcast_to(sums_ref[...].astype(out_ref.dtype)[None], out_ref.shape)


def first_kernel(order_ref, parts_ref, *refs):
    pairs = CHUNKS // 2
    kernel_ref, passage_ref, centroid_ref, out_ref, sums_ref, sems = refs[pairs:]
    copies = [
        pltpu.make_async_copy(ref, kernel_ref.at[pl.ds(2 * pair, 2)], sems.at[pair])
        for pair, ref in enumerate(refs[:pairs])
    ]
    for copy in copies:
        copy.start()
    parts = parts_ref[...]
    top = jnp.max(parts, axis=0)
    passage_ref[...] = -math.log(PASSAGES) - (
        top + jnp.log(jnp.sum(jnp.exp(parts - top[None]), axis=0))
    )
    peak = None
    for k in range(CHUNKS):
        if k % 2 == 0:
            copies[k // 2].wait()
        terms = kernel_ref[k] + passage_ref[pl.ds(order_ref[k], 1), :]
        kernel_ref[k] = terms
        peak = terms if peak is None else jnp.maximum(peak, terms)
    peak = jnp.max(peak, axis=1, keepdims=True)
    total = None
    for k in range(CHUNKS):
        terms = jnp.exp(kernel_ref[k] - peak)
        kernel_ref[k] = terms
        total = terms if total is None else total + terms
    total = jnp.sum(total, axis=1, keepdims=True)
    centroid_ref[...] = -math.log(CENTROIDS) - (peak + jnp.log(total))
    inverse = 1.0 / total
    for k in range(CHUNKS):
        terms = kernel_ref[k] * inverse
        kernel_ref[k] = terms
        sums_ref[pl.ds(order_ref[k], 1), :] = jnp.sum(terms, axis=0, keepdims=True)
    send_sums(sums_ref, out_ref)


def row_scale_of(parts_ref):
    parts = parts_ref[...].astype(jnp.float32)
    return (CENTROIDS / PASSAGES) / jnp.sum(parts, axis=0)


def column_sums(order_ref, kernel_ref, scale_ref):
    total = None
    for k in range(CHUNKS):
        terms = kernel_ref[k] * scale_ref[pl.ds(order_ref[k], 1), :]
        total = terms if total is None else total + terms
    return jnp.sum(total, axis=1, keepdims=True)


def middle_kernel(order_ref, parts_ref, kernel_ref, out_ref, sums_ref):
    sums_ref[...] = row_scale_of(parts_ref)
    scale = 1.0 / column_sums(order_ref, kernel_ref, sums_ref)
    for k in range(CHUNKS):
        sums_ref[pl.ds(order_ref[k], 1), :] = jnp.sum(
            kernel_ref[k] * scale, axis=0, keepdims=True
        )
    send_sums(sums_ref, out_ref)


def last_kernel(order_ref, parts_ref, kernel_ref, passage_ref, centroid_ref, *refs):
    chunk_refs = refs[:CHUNKS]
    new_ref, own_ref, duals_ref, weight_ref, held_ref, tile_ref, scale_ref, sems, out_sems = refs[CHUNKS:]
    span = chunk_refs[0].shape[0]
    tiles = held_ref.shape[0]
    for tile in range(tiles):
        for k in range(CHUNKS):
            pltpu.make_async_copy(
                chunk_refs[k].at[:, pl.ds(tile * WIDTH, WIDTH)],
                held_ref.at[tile, pl.ds(k * span, span), :],
                sems.at[tile],
            ).start()

    scale_ref[...] = row_scale_of(parts_ref)
    total = column_sums(order_ref, kernel_ref, scale_ref)
    inverse = 1.0 / total
    for k in range(CHUNKS):
        weight_ref[:, k * span : (k + 1) * span] = (
            kernel_ref[k] * scale_ref[pl.ds(order_ref[k], 1), :] * inverse
        ).astype(weight_ref.dtype)

    duals = centroid_ref[...] - jnp.log(total)
    square = (LANES, LANES)
    diagonal = lax.broadcasted_iota(jnp.int32, square, 0) == lax.broadcasted_iota(
        jnp.int32, square, 1
    )
    for k in range(duals.shape[0] // LANES):
        column = jnp.broadcast_to(duals[k * LANES : (k + 1) * LANES], square)
        duals_ref[pl.ds(k, 1), :] = jnp.sum(
            jnp.where(diagonal, column, 0.0), axis=0, keepdims=True
        )
    scale_ref[...] = passage_ref[...] + jnp.log(scale_ref[...])
    own_ref[...] = pltpu.roll(
        scale_ref[pl.ds(order_ref[CHUNKS], 1), :], LANES - order_ref[CHUNKS + 1], 1
    )

    def copy_out(tile):
        return pltpu.make_async_copy(
            tile_ref.at[tile % 2], new_ref.at[:, pl.ds(tile * WIDTH, WIDTH)], out_sems.at[tile % 2]
        )

    for tile in range(tiles):
        pltpu.make_async_copy(held_ref.at[tile], held_ref.at[tile], sems.at[tile]).wait()
        block = jnp.dot(
            weight_ref[...], held_ref[tile], preferred_element_type=jnp.float32
        ).astype(new_ref.dtype)
        if tile >= 2:
            copy_out(tile - 2).wait()
        tile_ref[tile % 2] = block
        copy_out(tile).start()
    for tile in range(tiles - 2, tiles):
        copy_out(tile).wait()


SMEM = pl.BlockSpec(memory_space=pltpu.SMEM)
VMEM = pl.BlockSpec(memory_space=pltpu.VMEM)
ANY = pl.BlockSpec(memory_space=pl.ANY)
LIMIT = pltpu.CompilerParams(vmem_limit_bytes=16 * 2**20)


def body(passages, centroids, dual_init):
    depth = passages.shape[1]
    local_rows = passages.shape[0]
    count = centroids.shape[0]
    factor = 4.0 / math.sqrt(depth)
    devices = lax.axis_size(EVERY)
    z, h, x, _, c = coords(lax.axis_index(EVERY))
    first = jnp.where(c == 0, x, z)
    second = jnp.where(c == 0, z, x)

    def fetch(step):
        def target(z, h, x, l, c):
            stays = h == c
            if stays and step == 0:
                return None
            h, c = (h, c) if stays else (1 - h, 1 - c)
            return (z, h, x - step, l, c) if c == 0 else (z - step, h, x, l, c)

        return move(passages, target)

    ring = [jnp.where(h == c, passages, fetch(0)), fetch(1), fetch(2), fetch(3)]
    ring = turned(jnp.stack(ring), first).reshape(4 * local_rows, depth)
    own = [ring, along_second(ring, -1), along_second(ring, 2), along_second(ring, 1)]
    order = [c * 4 + (second + k) % 4 for k in range(4)]
    order += [(1 - c) * 4 + (first + k) % 4 for k in range(4)]
    order = [order[k] for k in SLOTS]
    row, lane = jnp.where(h == 0, z, 4 + x), jnp.where(h == 0, x, z) * local_rows
    order = jnp.stack(order + [row, lane]).astype(jnp.int32)

    logits_of = functools.partial(
        pair_logits, factor, order, dual_init.reshape(count, 1), centroids
    )
    sibling = [None] * 4
    sibling[0] = to_sibling(own[0])
    pairs = [logits_of(own[0], sibling[0])]
    own[1], own[2], own[3], _ = lax.optimization_barrier((own[1], own[2], own[3], pairs[0]))
    sibling[3] = to_sibling(own[3])
    sibling[2] = to_sibling(own[2])
    sibling[1] = to_sibling(own[1])
    pairs.append(logits_of(own[2], own[1]))
    sibling[3], sibling[2], _ = lax.optimization_barrier((sibling[3], sibling[2], pairs[1]))
    pairs.append(logits_of(own[3], sibling[3]))
    sibling[1], sibling[2], _ = lax.optimization_barrier((sibling[1], sibling[2], pairs[2]))
    pairs.append(logits_of(sibling[2], sibling[1], [logsum for _, logsum in pairs]))
    chunks = own + sibling
    chunks = [chunks[k] for k in SLOTS]
    logits = [pair[0] for pair in pairs]
    span = chunks[0].shape[0]
    f32 = jnp.float32
    parts = to_every(pairs[-1][1])

    sent = jax.ShapeDtypeStruct((devices, CHUNKS, span), jnp.bfloat16)
    block = pl.BlockSpec((devices, CHUNKS, span), lambda: (0, 0, 0))
    sums = pltpu.VMEM((CHUNKS, span), f32)
    kernel, passage_first, centroid_first, partial = pl.pallas_call(
        first_kernel,
        in_specs=[SMEM, VMEM] + [ANY] * len(logits),
        out_specs=[VMEM] * 3 + [block],
        out_shape=[
            jax.ShapeDtypeStruct((CHUNKS, count, span), f32),
            jax.ShapeDtypeStruct((CHUNKS, span), f32),
            jax.ShapeDtypeStruct((count, 1), f32),
            sent,
        ],
        scratch_shapes=[sums, pltpu.SemaphoreType.DMA((len(logits),))],
        compiler_params=LIMIT,
    )(order, parts, *logits)
    partial = pl.pallas_call(
        middle_kernel,
        in_specs=[SMEM, VMEM, VMEM],
        out_specs=block,
        out_shape=sent,
        scratch_shapes=[sums],
        compiler_params=LIMIT,
    )(order, to_every(partial), kernel)
    new_centroids, own_duals, centroid_duals = pl.pallas_call(
        last_kernel,
        in_specs=[SMEM] + [VMEM] * 4 + [ANY] * CHUNKS,
        out_specs=[ANY, VMEM, VMEM],
        out_shape=[
            jax.ShapeDtypeStruct((count, depth), jnp.bfloat16),
            jax.ShapeDtypeStruct((1, span), f32),
            jax.ShapeDtypeStruct((count // LANES, LANES), f32),
        ],
        scratch_shapes=[
            pltpu.VMEM((count, CHUNKS * span), jnp.bfloat16),
            pltpu.VMEM((depth // WIDTH, CHUNKS * span, WIDTH), jnp.bfloat16),
            pltpu.VMEM((2, count, WIDTH), jnp.bfloat16),
            sums,
            pltpu.SemaphoreType.DMA((depth // WIDTH,)),
            pltpu.SemaphoreType.DMA((2,)),
        ],
        compiler_params=pltpu.CompilerParams(vmem_limit_bytes=24 * 2**20),
    )(order, to_every(partial), kernel, passage_first, centroid_first, *chunks)
    own_duals = own_duals[0, :local_rows]
    return (new_centroids, own_duals, centroid_duals.reshape(count))


def solution(mesh):
    in_specs = (P("psg", None), P(("psg", "cen"), None), P(("psg", "cen")))
    out_specs = (P(("psg", "cen"), None), P("psg"), P(("psg", "cen")))
    return jax.shard_map(body, mesh=mesh, in_specs=in_specs, out_specs=out_specs, check_vma=False)
```

```python
import functools
import math

import jax
import jax.numpy as jnp
from jax import lax
from jax.experimental import pallas as pl
from jax.experimental.pallas import tpu as pltpu
from jax.sharding import PartitionSpec as P

CENTROIDS = 65536
PASSAGES = 1024
EVERY = ("psg", "cen")
X, Z, HALVES = 4, 4, 2
CHUNKS = 8
OWN = (0, 3, 2, 1)
LANES = 128
WIDTH = 1024


def coords(device):
    return (
        device // (HALVES * X * 4),
        device // (X * 4) % HALVES,
        device // 4 % X,
        device // 2 % 2,
        device % 2,
    )


def move(value, target):
    pairs = []
    for device in range(Z * HALVES * X * 4):
        there = target(*coords(device))
        if there is not None:
            z, h, x, l, c = there
            pairs.append((device, (((z % Z) * HALVES + h) * X + x % X) * 4 + l * 2 + c))
    return lax.ppermute(value, EVERY, pairs)


def along_second(value, step):
    return move(
        value,
        lambda z, h, x, l, c: (z + step, h, x, l, c) if c == 0 else (z, h, x + step, l, c),
    )


def to_sibling(value):
    return move(value, lambda z, h, x, l, c: (z, h, x, l, 1 - c))


def to_every(copies):
    return lax.all_to_all(copies, EVERY, 0, 0)


def turned(rows, places):
    return lax.dynamic_slice_in_dim(jnp.concatenate([rows, rows], 0), 4 - places, 4, 0)


def logits_kernel(factor, count, order_ref, *refs):
    duals_refs, centroids_refs = refs[:2], refs[2:4]
    chunk_refs, earlier = refs[4 : 4 + count], refs[4 + count : -4]
    logits_refs, out_ref, rows_ref = refs[-4:-2], refs[-2], refs[-1]
    chunks = jnp.concatenate([ref[...] for ref in chunk_refs], axis=0)
    tops, totals = [], []
    for duals_ref, centroids_ref, logits_ref in zip(duals_refs, centroids_refs, logits_refs):
        product = factor * lax.dot_general(
            centroids_ref[...], chunks, (((1,), (1,)), ((), ())), preferred_element_type=jnp.float32
        )
        for k in range(count):
            logits_ref[k] = product[:, k * LANES : (k + 1) * LANES]
        shifted = product + duals_ref[...]
        top = jnp.max(shifted, axis=0, keepdims=True)
        tops.append(top)
        totals.append(jnp.sum(jnp.exp(shifted - top), axis=0, keepdims=True))
    top = jnp.maximum(*tops)
    logsum = top + jnp.log(sum(total * jnp.exp(own - top) for own, total in zip(tops, totals)))
    logsums = [logsum[:, k * LANES : (k + 1) * LANES] for k in range(count)]
    if not earlier:
        for k in range(count):
            out_ref[k : k + 1, :] = logsums[k]
        return
    logsums = [earlier[0][k : k + 1, :] for k in range(4 - count)] + logsums
    for slot in range(4):
        rows_ref[pl.ds(lax.rem(order_ref[slot], 4), 1), :] = logsums[slot]
    send_sums(rows_ref, out_ref)


def held(array):
    return pltpu.with_memory_space_constraint(array, pltpu.VMEM)


def chunk_logits(factor, order, duals, centroids, chunks, earlier=()):
    rows = centroids[0].shape[0]
    devices = lax.axis_size(EVERY)
    f32 = jnp.float32
    if earlier:
        out_spec = pl.BlockSpec((devices, 4, LANES), lambda: (0, 0, 0))
        out = jax.ShapeDtypeStruct((devices, 4, LANES), f32)
    else:
        out_spec, out = VMEM, jax.ShapeDtypeStruct((len(chunks), LANES), f32)
    logits = jax.ShapeDtypeStruct((len(chunks), rows, LANES), f32)
    block = pl.BlockSpec(logits.shape, lambda: (0, 0, 0))
    return pl.pallas_call(
        functools.partial(logits_kernel, factor, len(chunks)),
        in_specs=[SMEM] + [VMEM] * (4 + len(chunks) + len(earlier)),
        out_specs=[block, block, out_spec],
        out_shape=[logits, logits, out],
        scratch_shapes=[pltpu.VMEM((4, LANES), f32)],
        compiler_params=LIMIT,
    )(order, *duals, *[held(array) for array in (*centroids, *chunks)], *earlier)


def send_sums(sums_ref, out_ref):
    out_ref[...] = jnp.broadcast_to(sums_ref[...].astype(out_ref.dtype)[None], out_ref.shape)


def first_kernel(order_ref, parts_ref, *refs):
    logits_refs = refs[:4]
    kernel_ref, passage_ref, centroid_ref, out_ref, sums_ref, sems = refs[4:]
    starts = (0, 1, 4, 5)
    copies = [
        pltpu.make_async_copy(ref, kernel_ref.at[pl.ds(start, ref.shape[0])], sems.at[number])
        for number, (ref, start) in enumerate(zip(logits_refs, starts))
    ]
    for copy in copies:
        copy.start()
    parts = parts_ref[...].reshape(parts_ref.shape[0] // 2, 2, 4, LANES)
    for core in range(2):
        part = parts[:, core]
        top = jnp.max(part, axis=0)
        passage_ref[core * 4 : core * 4 + 4, :] = -math.log(PASSAGES) - (
            top + jnp.log(jnp.sum(jnp.exp(part - top[None]), axis=0))
        )
    peak = None
    for k in range(CHUNKS):
        if k in starts:
            copies[starts.index(k)].wait()
        terms = kernel_ref[k] + passage_ref[pl.ds(order_ref[k], 1), :]
        kernel_ref[k] = terms
        peak = terms if peak is None else jnp.maximum(peak, terms)
    peak = jnp.max(peak, axis=1, keepdims=True)
    total = None
    for k in range(CHUNKS):
        terms = jnp.exp(kernel_ref[k] - peak)
        kernel_ref[k] = terms
        total = terms if total is None else total + terms
    total = jnp.sum(total, axis=1, keepdims=True)
    centroid_ref[...] = -math.log(CENTROIDS) - (peak + jnp.log(total))
    inverse = 1.0 / total
    for k in range(CHUNKS):
        terms = kernel_ref[k] * inverse
        kernel_ref[k] = terms
        sums_ref[pl.ds(order_ref[k], 1), :] = jnp.sum(terms, axis=0, keepdims=True)
    send_sums(sums_ref, out_ref)


def row_scale_of(parts_ref):
    parts = parts_ref[...].astype(jnp.float32)
    return (CENTROIDS / PASSAGES) / jnp.sum(parts, axis=0)


def column_sums(order_ref, kernel_ref, scale_ref):
    total = None
    for k in range(CHUNKS):
        terms = kernel_ref[k] * scale_ref[pl.ds(order_ref[k], 1), :]
        total = terms if total is None else total + terms
    return jnp.sum(total, axis=1, keepdims=True)


def middle_kernel(order_ref, parts_ref, kernel_ref, out_ref, sums_ref):
    sums_ref[...] = row_scale_of(parts_ref)
    scale = 1.0 / column_sums(order_ref, kernel_ref, sums_ref)
    for k in range(CHUNKS):
        sums_ref[pl.ds(order_ref[k], 1), :] = jnp.sum(
            kernel_ref[k] * scale, axis=0, keepdims=True
        )
    send_sums(sums_ref, out_ref)


def last_kernel(order_ref, parts_ref, kernel_ref, passage_ref, centroid_ref, *refs):
    chunk_refs = refs[:CHUNKS]
    new_ref, own_ref, duals_ref, weight_ref, held_ref, tile_ref, scale_ref, sems, out_sems = refs[CHUNKS:]
    span = chunk_refs[0].shape[0]
    tiles = held_ref.shape[0]
    for tile in range(tiles):
        for k in range(CHUNKS):
            pltpu.make_async_copy(
                chunk_refs[k].at[:, pl.ds(tile * WIDTH, WIDTH)],
                held_ref.at[tile, pl.ds(k * span, span), :],
                sems.at[tile],
            ).start()

    scale_ref[...] = row_scale_of(parts_ref)
    total = column_sums(order_ref, kernel_ref, scale_ref)
    inverse = 1.0 / total
    for k in range(CHUNKS):
        weight_ref[:, k * span : (k + 1) * span] = (
            kernel_ref[k] * scale_ref[pl.ds(order_ref[k], 1), :] * inverse
        ).astype(weight_ref.dtype)

    def copy_out(tile):
        return pltpu.make_async_copy(
            tile_ref.at[tile % 2], new_ref.at[:, pl.ds(tile * WIDTH, WIDTH)], out_sems.at[tile % 2]
        )

    for tile in range(tiles):
        pltpu.make_async_copy(held_ref.at[tile], held_ref.at[tile], sems.at[tile]).wait()
        block = jnp.dot(
            weight_ref[...], held_ref[tile], preferred_element_type=jnp.float32
        ).astype(new_ref.dtype)
        if tile == 0:
            duals = centroid_ref[...] - jnp.log(total)
            square = (LANES, LANES)
            diagonal = lax.broadcasted_iota(jnp.int32, square, 0) == lax.broadcasted_iota(
                jnp.int32, square, 1
            )
            for k in range(duals.shape[0] // LANES):
                column = jnp.broadcast_to(duals[k * LANES : (k + 1) * LANES], square)
                duals_ref[pl.ds(k, 1), :] = jnp.sum(
                    jnp.where(diagonal, column, 0.0), axis=0, keepdims=True
                )
            scale_ref[...] = passage_ref[...] + jnp.log(scale_ref[...])
            own = pltpu.roll(scale_ref[pl.ds(order_ref[CHUNKS], 1), :], LANES - order_ref[CHUNKS + 1], 1)
            own_ref[...] = own[:, : own_ref.shape[1]]
        if tile >= 2:
            copy_out(tile - 2).wait()
        tile_ref[tile % 2] = block
        copy_out(tile).start()
    for tile in range(tiles - 2, tiles):
        copy_out(tile).wait()


SMEM = pl.BlockSpec(memory_space=pltpu.SMEM)
VMEM = pl.BlockSpec(memory_space=pltpu.VMEM)
ANY = pl.BlockSpec(memory_space=pl.ANY)
LIMIT = pltpu.CompilerParams(vmem_limit_bytes=16 * 2**20)


def body(passages, centroids, dual_init):
    depth = passages.shape[1]
    local_rows = passages.shape[0]
    count = centroids.shape[0]
    factor = 4.0 / math.sqrt(depth)
    devices = lax.axis_size(EVERY)
    z, h, x, _, c = coords(lax.axis_index(EVERY))
    first = jnp.where(c == 0, x, z)
    second = jnp.where(c == 0, z, x)

    def fetch(step):
        def target(z, h, x, l, c):
            stays = h == c
            if stays and step == 0:
                return None
            h, l, c = (h, l, c) if stays else (1 - h, 1 - l, 1 - c)
            return (z, h, x - step, l, c) if c == 0 else (z - step, h, x, l, c)

        return move(passages, target)

    ring = [jnp.where(h == c, passages, fetch(0)), fetch(1), fetch(2), fetch(3)]
    ring = turned(jnp.stack(ring), first).reshape(4 * local_rows, depth)
    own = [ring, along_second(ring, -1), along_second(ring, 2), along_second(ring, 1)]
    order = [c * 4 + (second + k) % 4 for k in OWN]
    order += [(1 - c) * 4 + (first + k) % 4 for k in OWN]
    row, lane = jnp.where(h == 0, z, 4 + x), jnp.where(h == 0, x, z) * local_rows
    order = jnp.stack(order + [row, lane]).astype(jnp.int32)

    column = lambda duals: duals.reshape(count, 1)
    logits_of = functools.partial(
        chunk_logits,
        factor,
        order,
        (column(dual_init), column(to_sibling(dual_init))),
        (centroids, to_sibling(centroids)),
    )
    groups = [logits_of((own[0],))]
    own[1], own[2], own[3], _ = lax.optimization_barrier((*own[1:], groups[0]))
    groups.append(logits_of([own[k] for k in OWN[1:]], earlier=[groups[0][2]]))
    own = [own[k] for k in OWN]
    logits = [group[0] for group in groups] + [to_sibling(group[1]) for group in groups]
    span = LANES
    f32 = jnp.float32
    parts = to_every(groups[-1][2])
    pieces = own + [to_sibling(chunk) for chunk in own]

    sent = jax.ShapeDtypeStruct((devices, CHUNKS, span), jnp.bfloat16)
    block = pl.BlockSpec((devices, CHUNKS, span), lambda: (0, 0, 0))
    sums = pltpu.VMEM((CHUNKS, span), f32)
    kernel, passage_first, centroid_first, partial = pl.pallas_call(
        first_kernel,
        in_specs=[SMEM, VMEM] + [ANY] * len(logits),
        out_specs=[VMEM] * 3 + [block],
        out_shape=[
            jax.ShapeDtypeStruct((CHUNKS, count, span), f32),
            jax.ShapeDtypeStruct((CHUNKS, span), f32),
            jax.ShapeDtypeStruct((count, 1), f32),
            sent,
        ],
        scratch_shapes=[sums, pltpu.SemaphoreType.DMA((len(logits),))],
        compiler_params=LIMIT,
    )(order, parts, *logits)
    partial, *pieces = lax.optimization_barrier((partial, *pieces))
    partial = pl.pallas_call(
        middle_kernel,
        in_specs=[SMEM, VMEM, VMEM],
        out_specs=block,
        out_shape=sent,
        scratch_shapes=[sums],
        compiler_params=LIMIT,
    )(order, to_every(partial), kernel)
    new_centroids, own_duals, centroid_duals = pl.pallas_call(
        last_kernel,
        in_specs=[SMEM] + [VMEM] * 4 + [ANY] * CHUNKS,
        out_specs=[ANY, VMEM, VMEM],
        out_shape=[
            jax.ShapeDtypeStruct((count, depth), jnp.bfloat16),
            jax.ShapeDtypeStruct((1, local_rows), f32),
            jax.ShapeDtypeStruct((count // LANES, LANES), f32),
        ],
        scratch_shapes=[
            pltpu.VMEM((count, CHUNKS * span), jnp.bfloat16),
            pltpu.VMEM((depth // WIDTH, CHUNKS * span, WIDTH), jnp.bfloat16),
            pltpu.VMEM((2, count, WIDTH), jnp.bfloat16),
            sums,
            pltpu.SemaphoreType.DMA((depth // WIDTH,)),
            pltpu.SemaphoreType.DMA((2,)),
        ],
        compiler_params=pltpu.CompilerParams(vmem_limit_bytes=24 * 2**20),
    )(order, to_every(partial), kernel, passage_first, centroid_first, *pieces)
    own_duals = own_duals.reshape(local_rows)
    return (new_centroids, own_duals, centroid_duals.reshape(count))


def solution(mesh):
    in_specs = (P("psg", None), P(("psg", "cen"), None), P(("psg", "cen")))
    out_specs = (P(("psg", "cen"), None), P("psg"), P(("psg", "cen")))
    return jax.shard_map(body, mesh=mesh, in_specs=in_specs, out_specs=out_specs, check_vma=False)
```

```python
import functools
import math

import jax
import jax.numpy as jnp
from jax import lax
from jax.experimental import pallas as pl
from jax.experimental.pallas import tpu as pltpu
from jax.sharding import PartitionSpec as P

CENTROIDS = 65536
PASSAGES = 1024
EVERY = ("psg", "cen")
X, Z, HALVES = 4, 4, 2
CHUNKS = 8
OWN = (0, 3, 2, 1)
LANES = 128
WIDTH = 2048
PARTS = 16


def coords(device):
    return (
        device // (HALVES * X * 4),
        device // (X * 4) % HALVES,
        device // 4 % X,
        device // 2 % 2,
        device % 2,
    )


def move(value, target):
    pairs = []
    for device in range(Z * HALVES * X * 4):
        there = target(*coords(device))
        if there is not None:
            z, h, x, l, c = there
            pairs.append((device, (((z % Z) * HALVES + h) * X + x % X) * 4 + l * 2 + c))
    return lax.ppermute(value, EVERY, pairs)


def along_second(value, step):
    return move(
        value,
        lambda z, h, x, l, c: (z + step, h, x, l, c) if c == 0 else (z, h, x + step, l, c),
    )


def to_sibling(value):
    return move(value, lambda z, h, x, l, c: (z, h, x, l, 1 - c))


def to_every(copies):
    return lax.all_to_all(copies, EVERY, 0, 0)


def turned(rows, places):
    return lax.dynamic_slice_in_dim(jnp.concatenate([rows, rows], 0), 4 - places, 4, 0)


def logits_kernel(factor, count, order_ref, *refs):
    duals_refs, centroids_refs = refs[:2], refs[2:4]
    chunk_refs, refs = refs[4 : 4 + count], refs[4 + count :]
    if count == 1:
        earlier, (*logits_refs, out_ref, near_ref, sem) = None, refs
        size = near_ref.shape[0] // PARTS
        for part in range(PARTS):
            rows = pl.ds(part * size, size)
            pltpu.make_async_copy(centroids_refs[1].at[rows], near_ref.at[rows], sem).start()
        centroids_refs = centroids_refs[0], near_ref
    else:
        earlier, *logits_refs, out_ref, rows_ref = refs
    chunks = jnp.concatenate([ref[...] for ref in chunk_refs], axis=0)
    tops, totals = [], []
    for duals_ref, centroids_ref, logits_ref in zip(duals_refs, centroids_refs, logits_refs):
        if count == 1 and centroids_ref is near_ref:
            pltpu.make_async_copy(near_ref, near_ref, sem).wait()
        product = factor * lax.dot_general(
            centroids_ref[...], chunks, (((1,), (1,)), ((), ())), preferred_element_type=jnp.float32
        )
        for k in range(count):
            logits_ref[k] = product[:, k * LANES : (k + 1) * LANES]
        shifted = product + duals_ref[...]
        top = jnp.max(shifted, axis=0, keepdims=True)
        tops.append(top)
        totals.append(jnp.sum(jnp.exp(shifted - top), axis=0, keepdims=True))
    top = jnp.maximum(*tops)
    logsum = top + jnp.log(sum(total * jnp.exp(own - top) for own, total in zip(tops, totals)))
    if earlier is None:
        out_ref[...] = logsum
        return
    logsums = [earlier[...]] + [logsum[:, k * LANES : (k + 1) * LANES] for k in range(count)]
    for slot in range(4):
        rows_ref[pl.ds(lax.rem(order_ref[slot], 4), 1), :] = logsums[slot]
    send_sums(rows_ref, out_ref)


def held(array):
    return pltpu.with_memory_space_constraint(array, pltpu.VMEM)


def chunk_logits(factor, order, duals, centroids, chunks, earlier=()):
    rows = centroids[0].shape[0]
    devices = lax.axis_size(EVERY)
    f32 = jnp.float32
    logits = jax.ShapeDtypeStruct((len(chunks), rows, LANES), f32)
    block = pl.BlockSpec(logits.shape, lambda: (0, 0, 0))
    if earlier:
        second = VMEM
        out_specs = [pl.BlockSpec((devices, 4, LANES), lambda: (0, 0, 0))]
        outs = [jax.ShapeDtypeStruct((devices, 4, LANES), f32)]
        scratch = [pltpu.VMEM((4, LANES), f32)]
    else:
        second, out_specs = ANY, [VMEM, VMEM]
        outs = [jax.ShapeDtypeStruct((1, LANES), f32)]
        outs += [jax.ShapeDtypeStruct(centroids[1].shape, centroids[1].dtype)]
        scratch = [pltpu.SemaphoreType.DMA]
    near = [held(array) for array in chunks]
    return pl.pallas_call(
        functools.partial(logits_kernel, factor, len(chunks)),
        in_specs=[SMEM] + [VMEM] * 3 + [second] + [VMEM] * (len(chunks) + len(earlier)),
        out_specs=[block, block] + out_specs,
        out_shape=[logits, logits] + outs,
        scratch_shapes=scratch,
        compiler_params=LIMIT,
    )(order, *duals, held(centroids[0]), centroids[1], *near, *earlier)


def send_sums(sums_ref, out_ref):
    out_ref[...] = jnp.broadcast_to(sums_ref[...].astype(out_ref.dtype)[None], out_ref.shape)


def first_kernel(order_ref, parts_ref, *refs):
    logits_refs = refs[:4]
    kernel_ref, passage_ref, centroid_ref, out_ref, sums_ref, sems = refs[4:]
    starts = (0, 1, 4, 5)
    copies = [
        pltpu.make_async_copy(ref, kernel_ref.at[pl.ds(start, ref.shape[0])], sems.at[number])
        for number, (ref, start) in enumerate(zip(logits_refs, starts))
    ]
    for copy in copies:
        copy.start()
    parts = parts_ref[...].reshape(parts_ref.shape[0] // 2, 2, 4, LANES)
    for core in range(2):
        part = parts[:, core]
        top = jnp.max(part, axis=0)
        passage_ref[core * 4 : core * 4 + 4, :] = -math.log(PASSAGES) - (
            top + jnp.log(jnp.sum(jnp.exp(part - top[None]), axis=0))
        )
    peak = None
    for k in range(CHUNKS):
        if k in starts:
            copies[starts.index(k)].wait()
        terms = kernel_ref[k] + passage_ref[pl.ds(order_ref[k], 1), :]
        kernel_ref[k] = terms
        peak = terms if peak is None else jnp.maximum(peak, terms)
    peak = jnp.max(peak, axis=1, keepdims=True)
    total = None
    for k in range(CHUNKS):
        terms = jnp.exp(kernel_ref[k] - peak)
        kernel_ref[k] = terms
        total = terms if total is None else total + terms
    total = jnp.sum(total, axis=1, keepdims=True)
    centroid_ref[...] = -math.log(CENTROIDS) - (peak + jnp.log(total))
    inverse = 1.0 / total
    for k in range(CHUNKS):
        terms = kernel_ref[k] * inverse
        kernel_ref[k] = terms
        sums_ref[pl.ds(order_ref[k], 1), :] = jnp.sum(terms, axis=0, keepdims=True)
    send_sums(sums_ref, out_ref)


def row_scale_of(parts_ref):
    parts = parts_ref[...].astype(jnp.float32)
    return (CENTROIDS / PASSAGES) / jnp.sum(parts, axis=0)


def column_sums(order_ref, kernel_ref, scale_ref):
    total = None
    for k in range(CHUNKS):
        terms = kernel_ref[k] * scale_ref[pl.ds(order_ref[k], 1), :]
        total = terms if total is None else total + terms
    return jnp.sum(total, axis=1, keepdims=True)


def middle_kernel(order_ref, parts_ref, kernel_ref, out_ref, sums_ref):
    sums_ref[...] = row_scale_of(parts_ref)
    scale = 1.0 / column_sums(order_ref, kernel_ref, sums_ref)
    for k in range(CHUNKS):
        sums_ref[pl.ds(order_ref[k], 1), :] = jnp.sum(
            kernel_ref[k] * scale, axis=0, keepdims=True
        )
    send_sums(sums_ref, out_ref)


def last_kernel(order_ref, parts_ref, kernel_ref, passage_ref, centroid_ref, *refs):
    chunk_refs = refs[:CHUNKS]
    new_ref, own_ref, duals_ref, weight_ref, held_ref, tile_ref, scale_ref, sems, out_sems = refs[CHUNKS:]
    span = chunk_refs[0].shape[0]
    tiles = held_ref.shape[0]
    for tile in range(tiles):
        for k in range(CHUNKS):
            pltpu.make_async_copy(
                chunk_refs[k].at[:, pl.ds(tile * WIDTH, WIDTH)],
                held_ref.at[tile, pl.ds(k * span, span), :],
                sems.at[tile],
            ).start()

    scale_ref[...] = row_scale_of(parts_ref)
    total = column_sums(order_ref, kernel_ref, scale_ref)
    inverse = 1.0 / total
    for k in range(CHUNKS):
        weight_ref[:, k * span : (k + 1) * span] = (
            kernel_ref[k] * scale_ref[pl.ds(order_ref[k], 1), :] * inverse
        ).astype(weight_ref.dtype)

    def copy_out(tile):
        return pltpu.make_async_copy(
            tile_ref.at[tile % 2], new_ref.at[:, pl.ds(tile * WIDTH, WIDTH)], out_sems.at[tile % 2]
        )

    for tile in range(tiles):
        pltpu.make_async_copy(held_ref.at[tile], held_ref.at[tile], sems.at[tile]).wait()
        block = jnp.dot(
            weight_ref[...], held_ref[tile], preferred_element_type=jnp.float32
        ).astype(new_ref.dtype)
        if tile == 0:
            duals = centroid_ref[...] - jnp.log(total)
            square = (LANES, LANES)
            diagonal = lax.broadcasted_iota(jnp.int32, square, 0) == lax.broadcasted_iota(
                jnp.int32, square, 1
            )
            for k in range(duals.shape[0] // LANES):
                column = jnp.broadcast_to(duals[k * LANES : (k + 1) * LANES], square)
                duals_ref[pl.ds(k, 1), :] = jnp.sum(
                    jnp.where(diagonal, column, 0.0), axis=0, keepdims=True
                )
            scale_ref[...] = passage_ref[...] + jnp.log(scale_ref[...])
            own = pltpu.roll(scale_ref[pl.ds(order_ref[CHUNKS], 1), :], LANES - order_ref[CHUNKS + 1], 1)
            own_ref[...] = own[:, : own_ref.shape[1]]
        if tile >= 2:
            copy_out(tile - 2).wait()
        tile_ref[tile % 2] = block
        copy_out(tile).start()
    for tile in range(tiles - 2, tiles):
        copy_out(tile).wait()


SMEM = pl.BlockSpec(memory_space=pltpu.SMEM)
VMEM = pl.BlockSpec(memory_space=pltpu.VMEM)
ANY = pl.BlockSpec(memory_space=pl.ANY)
LIMIT = pltpu.CompilerParams(vmem_limit_bytes=16 * 2**20)


def body(passages, centroids, dual_init):
    depth = passages.shape[1]
    local_rows = passages.shape[0]
    count = centroids.shape[0]
    factor = 4.0 / math.sqrt(depth)
    devices = lax.axis_size(EVERY)
    z, h, x, _, c = coords(lax.axis_index(EVERY))
    first = jnp.where(c == 0, x, z)
    second = jnp.where(c == 0, z, x)

    def fetch(step):
        def target(z, h, x, l, c):
            stays = h == c
            if stays and step == 0:
                return None
            h, l, c = (h, l, c) if stays else (1 - h, 1 - l, 1 - c)
            return (z, h, x - step, l, c) if c == 0 else (z - step, h, x, l, c)

        return move(passages, target)

    ring = [jnp.where(h == c, passages, fetch(0)), fetch(1), fetch(2), fetch(3)]
    ring = turned(jnp.stack(ring), first).reshape(4 * local_rows, depth)
    own = [ring, along_second(ring, -1), along_second(ring, 2), along_second(ring, 1)]
    order = [c * 4 + (second + k) % 4 for k in OWN]
    order += [(1 - c) * 4 + (first + k) % 4 for k in OWN]
    row, lane = jnp.where(h == 0, z, 4 + x), jnp.where(h == 0, x, z) * local_rows
    order = jnp.stack(order + [row, lane]).astype(jnp.int32)

    column = lambda duals: duals.reshape(count, 1)
    logits_of = functools.partial(
        chunk_logits, factor, order, (column(dual_init), column(to_sibling(dual_init)))
    )
    groups = [logits_of((centroids, to_sibling(centroids)), (own[0],))]
    own[1], own[2], own[3], _ = lax.optimization_barrier((*own[1:], groups[0]))
    groups.append(
        logits_of((centroids, groups[0][3]), [own[k] for k in OWN[1:]], earlier=[groups[0][2]])
    )
    own = [own[k] for k in OWN]
    logits = [group[0] for group in groups] + [to_sibling(group[1]) for group in groups]
    span = LANES
    f32 = jnp.float32
    parts = to_every(groups[-1][2])
    pieces = own + [to_sibling(chunk) for chunk in own]

    sent = jax.ShapeDtypeStruct((devices, CHUNKS, span), jnp.bfloat16)
    block = pl.BlockSpec((devices, CHUNKS, span), lambda: (0, 0, 0))
    sums = pltpu.VMEM((CHUNKS, span), f32)
    kernel, passage_first, centroid_first, partial = pl.pallas_call(
        first_kernel,
        in_specs=[SMEM, VMEM] + [ANY] * len(logits),
        out_specs=[VMEM] * 3 + [block],
        out_shape=[
            jax.ShapeDtypeStruct((CHUNKS, count, span), f32),
            jax.ShapeDtypeStruct((CHUNKS, span), f32),
            jax.ShapeDtypeStruct((count, 1), f32),
            sent,
        ],
        scratch_shapes=[sums, pltpu.SemaphoreType.DMA((len(logits),))],
        compiler_params=LIMIT,
    )(order, parts, *logits)
    partial, *pieces = lax.optimization_barrier((partial, *pieces))
    partial = pl.pallas_call(
        middle_kernel,
        in_specs=[SMEM, VMEM, VMEM],
        out_specs=block,
        out_shape=sent,
        scratch_shapes=[sums],
        compiler_params=LIMIT,
    )(order, to_every(partial), kernel)
    new_centroids, own_duals, centroid_duals = pl.pallas_call(
        last_kernel,
        in_specs=[SMEM] + [VMEM] * 4 + [ANY] * CHUNKS,
        out_specs=[ANY, VMEM, VMEM],
        out_shape=[
            jax.ShapeDtypeStruct((count, depth), jnp.bfloat16),
            jax.ShapeDtypeStruct((1, local_rows), f32),
            jax.ShapeDtypeStruct((count // LANES, LANES), f32),
        ],
        scratch_shapes=[
            pltpu.VMEM((count, CHUNKS * span), jnp.bfloat16),
            pltpu.VMEM((depth // WIDTH, CHUNKS * span, WIDTH), jnp.bfloat16),
            pltpu.VMEM((2, count, WIDTH), jnp.bfloat16),
            sums,
            pltpu.SemaphoreType.DMA((depth // WIDTH,)),
            pltpu.SemaphoreType.DMA((2,)),
        ],
        compiler_params=pltpu.CompilerParams(vmem_limit_bytes=24 * 2**20),
    )(order, to_every(partial), kernel, passage_first, centroid_first, *pieces)
    own_duals = own_duals.reshape(local_rows)
    return (new_centroids, own_duals, centroid_duals.reshape(count))


def solution(mesh):
    in_specs = (P("psg", None), P(("psg", "cen"), None), P(("psg", "cen")))
    out_specs = (P(("psg", "cen"), None), P("psg"), P(("psg", "cen")))
    return jax.shard_map(body, mesh=mesh, in_specs=in_specs, out_specs=out_specs, check_vma=False)
```

```python
import functools
import math

import jax
import jax.numpy as jnp
from jax import lax
from jax.experimental import pallas as pl
from jax.experimental.pallas import tpu as pltpu
from jax.sharding import PartitionSpec as P

CENTROIDS = 65536
PASSAGES = 1024
EVERY = ("psg", "cen")
X, Z, HALVES = 4, 4, 2
CHUNKS = 8
OWN = (0, 3, 2, 1)
LANES = 128
WIDTH = 2048
PARTS = 16


def coords(device):
    return (
        device // (HALVES * X * 4),
        device // (X * 4) % HALVES,
        device // 4 % X,
        device // 2 % 2,
        device % 2,
    )


def move(value, target):
    pairs = []
    for device in range(Z * HALVES * X * 4):
        there = target(*coords(device))
        if there is not None:
            z, h, x, l, c = there
            pairs.append((device, (((z % Z) * HALVES + h) * X + x % X) * 4 + l * 2 + c))
    return lax.ppermute(value, EVERY, pairs)


def along_second(value, step):
    return move(
        value,
        lambda z, h, x, l, c: (z + step, h, x, l, c) if c == 0 else (z, h, x + step, l, c),
    )


def to_sibling(value):
    return move(value, lambda z, h, x, l, c: (z, h, x, l, 1 - c))


def to_every(copies):
    return lax.all_to_all(copies, EVERY, 0, 0)


def turned(rows, places):
    return lax.dynamic_slice_in_dim(jnp.concatenate([rows, rows], 0), 4 - places, 4, 0)


def stage_kernel(*refs):
    rows_refs, centroids_refs, columns_refs, held_refs, sem = refs[:2], refs[2:4], refs[4:6], refs[6:8], refs[8]
    for source, target in zip(centroids_refs, held_refs):
        size = target.shape[0] // PARTS
        for part in range(PARTS):
            rows = pl.ds(part * size, size)
            pltpu.make_async_copy(source.at[rows], target.at[rows], sem).start()
    square = (LANES, LANES)
    diagonal = lax.broadcasted_iota(jnp.int32, square, 0) == lax.broadcasted_iota(
        jnp.int32, square, 1
    )
    for source, target in zip(rows_refs, columns_refs):
        for k in range(source.shape[0]):
            row = jnp.broadcast_to(source[k : k + 1, :], square)
            target[k * LANES : (k + 1) * LANES, :] = jnp.sum(
                jnp.where(diagonal, row, 0.0), axis=1, keepdims=True
            )
    for target in held_refs:
        pltpu.make_async_copy(target, target, sem).wait()


def logits_kernel(factor, order_ref, *refs):
    duals_refs, centroids_refs, piece_refs = refs[:2], refs[2:4], refs[4:11]
    *logits_refs, out_ref, arrived_ref, rows_ref, sem = refs[11:]
    start = 0
    for ref in piece_refs[1:]:
        size = ref.shape[0]
        pltpu.make_async_copy(ref, arrived_ref.at[pl.ds(start, size)], sem).start()
        start += size
    chunks = jnp.concatenate([ref[...] for ref in piece_refs], axis=0)
    tops, totals = [], []
    for duals_ref, centroids_ref, logits_ref in zip(duals_refs, centroids_refs, logits_refs):
        product = factor * lax.dot_general(
            centroids_ref[...], chunks, (((1,), (1,)), ((), ())), preferred_element_type=jnp.float32
        )
        for k in range(4):
            logits_ref[k] = product[:, k * LANES : (k + 1) * LANES]
        shifted = product + duals_ref[...]
        top = jnp.max(shifted, axis=0, keepdims=True)
        tops.append(top)
        totals.append(jnp.sum(jnp.exp(shifted - top), axis=0, keepdims=True))
    top = jnp.maximum(*tops)
    logsum = top + jnp.log(sum(total * jnp.exp(own - top) for own, total in zip(tops, totals)))
    for k in range(4):
        rows_ref[pl.ds(lax.rem(order_ref[k], 4), 1), :] = logsum[:, k * LANES : (k + 1) * LANES]
    send_sums(rows_ref, out_ref)
    pltpu.make_async_copy(arrived_ref, arrived_ref, sem).wait()


def held(array):
    return pltpu.with_memory_space_constraint(array, pltpu.VMEM)


def staged(duals, centroids):
    rows = centroids[0].shape[0]
    column = jax.ShapeDtypeStruct((rows, 1), jnp.float32)
    arrays = [jax.ShapeDtypeStruct(array.shape, array.dtype) for array in centroids]
    return pl.pallas_call(
        stage_kernel,
        in_specs=[VMEM] * 2 + [ANY] * 2,
        out_specs=[VMEM] * 4,
        out_shape=[column, column] + arrays,
        scratch_shapes=[pltpu.SemaphoreType.DMA],
        compiler_params=LIMIT,
    )(*[dual.reshape(rows // LANES, LANES) for dual in duals], *centroids)


def chunk_logits(factor, order, columns, centroids, pieces):
    rows, depth = centroids[0].shape
    devices = lax.axis_size(EVERY)
    f32 = jnp.float32
    logits = jax.ShapeDtypeStruct((4, rows, LANES), f32)
    block = pl.BlockSpec(logits.shape, lambda: (0, 0, 0))
    return pl.pallas_call(
        functools.partial(logits_kernel, factor),
        in_specs=[SMEM] + [VMEM] * (4 + len(pieces)),
        out_specs=[block, block, pl.BlockSpec((devices, 4, LANES), lambda: (0, 0, 0)), ANY],
        out_shape=[
            logits,
            logits,
            jax.ShapeDtypeStruct((devices, 4, LANES), f32),
            jax.ShapeDtypeStruct((3 * LANES, depth), pieces[0].dtype),
        ],
        scratch_shapes=[pltpu.VMEM((4, LANES), f32), pltpu.SemaphoreType.DMA],
        compiler_params=pltpu.CompilerParams(vmem_limit_bytes=24 * 2**20),
    )(order, *columns, *centroids, *[held(array) for array in pieces])


def send_sums(sums_ref, out_ref):
    out_ref[...] = jnp.broadcast_to(sums_ref[...].astype(out_ref.dtype)[None], out_ref.shape)


def first_kernel(order_ref, parts_ref, *refs):
    logits_refs = refs[:2]
    kernel_ref, passage_ref, centroid_ref, out_ref, sums_ref, sems = refs[2:]
    starts = (0, 4)
    copies = [
        pltpu.make_async_copy(ref, kernel_ref.at[pl.ds(start, ref.shape[0])], sems.at[number])
        for number, (ref, start) in enumerate(zip(logits_refs, starts))
    ]
    for copy in copies:
        copy.start()
    parts = parts_ref[...].reshape(parts_ref.shape[0] // 2, 2, 4, LANES)
    for core in range(2):
        part = parts[:, core]
        top = jnp.max(part, axis=0)
        passage_ref[core * 4 : core * 4 + 4, :] = -math.log(PASSAGES) - (
            top + jnp.log(jnp.sum(jnp.exp(part - top[None]), axis=0))
        )
    peak = None
    for k in range(CHUNKS):
        if k in starts:
            copies[starts.index(k)].wait()
        terms = kernel_ref[k] + passage_ref[pl.ds(order_ref[k], 1), :]
        kernel_ref[k] = terms
        peak = terms if peak is None else jnp.maximum(peak, terms)
    peak = jnp.max(peak, axis=1, keepdims=True)
    total = None
    for k in range(CHUNKS):
        terms = jnp.exp(kernel_ref[k] - peak)
        kernel_ref[k] = terms
        total = terms if total is None else total + terms
    total = jnp.sum(total, axis=1, keepdims=True)
    centroid_ref[...] = -math.log(CENTROIDS) - (peak + jnp.log(total))
    inverse = 1.0 / total
    for k in range(CHUNKS):
        terms = kernel_ref[k] * inverse
        kernel_ref[k] = terms
        sums_ref[pl.ds(order_ref[k], 1), :] = jnp.sum(terms, axis=0, keepdims=True)
    send_sums(sums_ref, out_ref)


def row_scale_of(parts_ref):
    parts = parts_ref[...].astype(jnp.float32)
    return (CENTROIDS / PASSAGES) / jnp.sum(parts, axis=0)


def column_sums(order_ref, kernel_ref, scale_ref):
    total = None
    for k in range(CHUNKS):
        terms = kernel_ref[k] * scale_ref[pl.ds(order_ref[k], 1), :]
        total = terms if total is None else total + terms
    return jnp.sum(total, axis=1, keepdims=True)


def middle_kernel(order_ref, parts_ref, kernel_ref, out_ref, sums_ref):
    sums_ref[...] = row_scale_of(parts_ref)
    scale = 1.0 / column_sums(order_ref, kernel_ref, sums_ref)
    for k in range(CHUNKS):
        sums_ref[pl.ds(order_ref[k], 1), :] = jnp.sum(
            kernel_ref[k] * scale, axis=0, keepdims=True
        )
    send_sums(sums_ref, out_ref)


def last_kernel(order_ref, parts_ref, kernel_ref, passage_ref, centroid_ref, *refs):
    *piece_refs, new_ref, own_ref, duals_ref = refs[:-6]
    weight_ref, held_ref, tile_ref, scale_ref, sems, out_sems = refs[-6:]
    span, tiles = LANES, held_ref.shape[0]
    for tile in range(tiles):
        start = 0
        for ref in piece_refs:
            size = ref.shape[0]
            pltpu.make_async_copy(
                ref.at[:, pl.ds(tile * WIDTH, WIDTH)],
                held_ref.at[tile, pl.ds(start, size), :],
                sems.at[tile],
            ).start()
            start += size

    scale_ref[...] = row_scale_of(parts_ref)
    total = column_sums(order_ref, kernel_ref, scale_ref)
    inverse = 1.0 / total
    for k in range(CHUNKS):
        weight_ref[:, k * span : (k + 1) * span] = (
            kernel_ref[k] * scale_ref[pl.ds(order_ref[k], 1), :] * inverse
        ).astype(weight_ref.dtype)

    def copy_out(tile):
        return pltpu.make_async_copy(
            tile_ref.at[tile % 2], new_ref.at[:, pl.ds(tile * WIDTH, WIDTH)], out_sems.at[tile % 2]
        )

    for tile in range(tiles):
        pltpu.make_async_copy(held_ref.at[tile], held_ref.at[tile], sems.at[tile]).wait()
        block = jnp.dot(
            weight_ref[...], held_ref[tile], preferred_element_type=jnp.float32
        ).astype(new_ref.dtype)
        if tile == 0:
            duals = centroid_ref[...] - jnp.log(total)
            square = (LANES, LANES)
            diagonal = lax.broadcasted_iota(jnp.int32, square, 0) == lax.broadcasted_iota(
                jnp.int32, square, 1
            )
            for k in range(duals.shape[0] // LANES):
                column = jnp.broadcast_to(duals[k * LANES : (k + 1) * LANES], square)
                duals_ref[pl.ds(k, 1), :] = jnp.sum(
                    jnp.where(diagonal, column, 0.0), axis=0, keepdims=True
                )
            scale_ref[...] = passage_ref[...] + jnp.log(scale_ref[...])
            own = pltpu.roll(scale_ref[pl.ds(order_ref[CHUNKS], 1), :], LANES - order_ref[CHUNKS + 1], 1)
            own_ref[...] = own[:, : own_ref.shape[1]]
        if tile >= 2:
            copy_out(tile - 2).wait()
        tile_ref[tile % 2] = block
        copy_out(tile).start()
    for tile in range(tiles - 2, tiles):
        copy_out(tile).wait()


SMEM = pl.BlockSpec(memory_space=pltpu.SMEM)
VMEM = pl.BlockSpec(memory_space=pltpu.VMEM)
ANY = pl.BlockSpec(memory_space=pl.ANY)
LIMIT = pltpu.CompilerParams(vmem_limit_bytes=16 * 2**20)


def body(passages, centroids, dual_init):
    depth = passages.shape[1]
    local_rows = passages.shape[0]
    count = centroids.shape[0]
    factor = 4.0 / math.sqrt(depth)
    devices = lax.axis_size(EVERY)
    z, h, x, _, c = coords(lax.axis_index(EVERY))
    first = jnp.where(c == 0, x, z)
    second = jnp.where(c == 0, z, x)

    def fetch(step):
        def target(z, h, x, l, c):
            stays = h == c
            if stays and step == 0:
                return None
            h, l, c = (h, l, c) if stays else (1 - h, 1 - l, 1 - c)
            return (z, h, x - step, l, c) if c == 0 else (z - step, h, x, l, c)

        return move(passages, target)

    ring = [jnp.where(h == c, passages, fetch(0)), fetch(1), fetch(2), fetch(3)]
    ring = turned(jnp.stack(ring), first).reshape(4 * local_rows, depth)
    near_duals = to_sibling(dual_init)
    ring, near_duals = lax.optimization_barrier((ring, near_duals))

    half = ring.shape[0] // 2
    top, bottom = ring[:half], ring[half:]
    top_before, bottom_after = along_second(top, 1), along_second(bottom, -1)
    bottom_before, top_after = along_second(bottom, 1), along_second(top, -1)
    top_across, bottom_across = along_second(top_before, 1), along_second(bottom_after, -1)
    arrived = [top_before, bottom_before, top_across, bottom_across, top_after, bottom_after]
    order = [c * 4 + (second + k) % 4 for k in OWN]
    order += [(1 - c) * 4 + (first + k) % 4 for k in OWN]
    row, lane = jnp.where(h == 0, z, 4 + x), jnp.where(h == 0, x, z) * local_rows
    order = jnp.stack(order + [row, lane]).astype(jnp.int32)

    pairs, _ = lax.optimization_barrier(
        ((dual_init, near_duals, centroids, to_sibling(centroids)), (top_before, bottom_after))
    )
    *columns, near, sibling = staged(pairs[:2], pairs[2:])
    arrived, near, sibling = lax.optimization_barrier((arrived, near, sibling))
    *logits, parts, arrived = chunk_logits(factor, order, columns, (near, sibling), [ring] + arrived)
    logits = [logits[0], to_sibling(logits[1])]
    span = LANES
    f32 = jnp.float32
    parts = to_every(parts)
    own = [ring, arrived]
    pieces = own + [to_sibling(chunk) for chunk in own]

    sent = jax.ShapeDtypeStruct((devices, CHUNKS, span), jnp.bfloat16)
    block = pl.BlockSpec((devices, CHUNKS, span), lambda: (0, 0, 0))
    sums = pltpu.VMEM((CHUNKS, span), f32)
    kernel, passage_first, centroid_first, partial = pl.pallas_call(
        first_kernel,
        in_specs=[SMEM, VMEM] + [ANY] * len(logits),
        out_specs=[VMEM] * 3 + [block],
        out_shape=[
            jax.ShapeDtypeStruct((CHUNKS, count, span), f32),
            jax.ShapeDtypeStruct((CHUNKS, span), f32),
            jax.ShapeDtypeStruct((count, 1), f32),
            sent,
        ],
        scratch_shapes=[sums, pltpu.SemaphoreType.DMA((len(logits),))],
        compiler_params=LIMIT,
    )(order, parts, *logits)
    partial, *pieces = lax.optimization_barrier((partial, *pieces))
    partial = pl.pallas_call(
        middle_kernel,
        in_specs=[SMEM, VMEM, VMEM],
        out_specs=block,
        out_shape=sent,
        scratch_shapes=[sums],
        compiler_params=LIMIT,
    )(order, to_every(partial), kernel)
    new_centroids, own_duals, centroid_duals = pl.pallas_call(
        last_kernel,
        in_specs=[SMEM] + [VMEM] * 4 + [ANY] * len(pieces),
        out_specs=[ANY, VMEM, VMEM],
        out_shape=[
            jax.ShapeDtypeStruct((count, depth), jnp.bfloat16),
            jax.ShapeDtypeStruct((1, local_rows), f32),
            jax.ShapeDtypeStruct((count // LANES, LANES), f32),
        ],
        scratch_shapes=[
            pltpu.VMEM((count, CHUNKS * span), jnp.bfloat16),
            pltpu.VMEM((depth // WIDTH, CHUNKS * span, WIDTH), jnp.bfloat16),
            pltpu.VMEM((2, count, WIDTH), jnp.bfloat16),
            sums,
            pltpu.SemaphoreType.DMA((depth // WIDTH,)),
            pltpu.SemaphoreType.DMA((2,)),
        ],
        compiler_params=pltpu.CompilerParams(vmem_limit_bytes=24 * 2**20),
    )(order, to_every(partial), kernel, passage_first, centroid_first, *pieces)
    own_duals = own_duals.reshape(local_rows)
    return (new_centroids, own_duals, centroid_duals.reshape(count))


def solution(mesh):
    in_specs = (P("psg", None), P(("psg", "cen"), None), P(("psg", "cen")))
    out_specs = (P(("psg", "cen"), None), P("psg"), P(("psg", "cen")))
    return jax.shard_map(body, mesh=mesh, in_specs=in_specs, out_specs=out_specs, check_vma=False)
```

```python
import functools
import math

import jax
import jax.numpy as jnp
from jax import lax
from jax.experimental import pallas as pl
from jax.experimental.pallas import tpu as pltpu
from jax.sharding import PartitionSpec as P

CENTROIDS = 65536
PASSAGES = 1024
EVERY = ("psg", "cen")
X, Z, HALVES = 4, 4, 2
CHUNKS = 8
OWN = (0, 3, 2, 1)
LANES = 128
WIDTH = 2048
PARTS = 16


def coords(device):
    return (
        device // (HALVES * X * 4),
        device // (X * 4) % HALVES,
        device // 4 % X,
        device // 2 % 2,
        device % 2,
    )


def move(value, target):
    pairs = []
    for device in range(Z * HALVES * X * 4):
        there = target(*coords(device))
        if there is not None:
            z, h, x, l, c = there
            pairs.append((device, (((z % Z) * HALVES + h) * X + x % X) * 4 + l * 2 + c))
    return lax.ppermute(value, EVERY, pairs)


def along_second(value, step):
    return move(
        value,
        lambda z, h, x, l, c: (z + step, h, x, l, c) if c == 0 else (z, h, x + step, l, c),
    )


def to_sibling(value):
    return move(value, lambda z, h, x, l, c: (z, h, x, l, 1 - c))


def to_every(copies):
    return lax.all_to_all(copies, EVERY, 0, 0)


def rolled(order_ref, first, rows):
    low = lax.broadcasted_iota(jnp.int32, rows.shape, 0) < 4
    return jnp.where(
        low, pltpu.roll(rows, order_ref[first], 1), pltpu.roll(rows, order_ref[first + 1], 1)
    )


def to_common(order_ref, rows):
    return rolled(order_ref, CHUNKS + 2, rows)


def to_local(order_ref, rows):
    return rolled(order_ref, CHUNKS + 4, rows)


def stage_kernel(*refs):
    rows_refs, centroids_refs, columns_refs, held_refs, sem = refs[:2], refs[2:4], refs[4:6], refs[6:8], refs[8]
    for source, target in zip(centroids_refs, held_refs):
        size = target.shape[0] // PARTS
        for part in range(PARTS):
            rows = pl.ds(part * size, size)
            pltpu.make_async_copy(source.at[rows], target.at[rows], sem).start()
    square = (LANES, LANES)
    diagonal = lax.broadcasted_iota(jnp.int32, square, 0) == lax.broadcasted_iota(
        jnp.int32, square, 1
    )
    for source, target in zip(rows_refs, columns_refs):
        for k in range(source.shape[0]):
            row = jnp.broadcast_to(source[k : k + 1, :], square)
            target[k * LANES : (k + 1) * LANES, :] = jnp.sum(
                jnp.where(diagonal, row, 0.0), axis=1, keepdims=True
            )
    for target in held_refs:
        pltpu.make_async_copy(target, target, sem).wait()


def logits_kernel(factor, order_ref, *refs):
    duals_refs, centroids_refs, piece_refs = refs[:2], refs[2:4], refs[4:12]
    *logits_refs, out_ref, arrived_ref, rows_ref, sem = refs[12:]
    start = 0
    for ref in piece_refs:
        size = ref.shape[0]
        pltpu.make_async_copy(ref, arrived_ref.at[pl.ds(start, size)], sem).start()
        start += size
    chunks = jnp.concatenate([ref[...] for ref in piece_refs], axis=0)
    tops, totals = [], []
    for duals_ref, centroids_ref, logits_ref in zip(duals_refs, centroids_refs, logits_refs):
        product = factor * lax.dot_general(
            centroids_ref[...], chunks, (((1,), (1,)), ((), ())), preferred_element_type=jnp.float32
        )
        for k in range(4):
            logits_ref[k] = product[:, k * LANES : (k + 1) * LANES]
        shifted = product + duals_ref[...]
        top = jnp.max(shifted, axis=0, keepdims=True)
        tops.append(top)
        totals.append(jnp.sum(jnp.exp(shifted - top), axis=0, keepdims=True))
    top = jnp.maximum(*tops)
    logsum = top + jnp.log(sum(total * jnp.exp(own - top) for own, total in zip(tops, totals)))
    for k in range(4):
        rows_ref[pl.ds(lax.rem(order_ref[k], 4), 1), :] = logsum[:, k * LANES : (k + 1) * LANES]
    core = lax.div(order_ref[0], 4)
    send_rows(pltpu.roll(rows_ref[...], order_ref[CHUNKS + 2 + core], 1), out_ref)
    pltpu.make_async_copy(arrived_ref, arrived_ref, sem).wait()


def held(array):
    return pltpu.with_memory_space_constraint(array, pltpu.VMEM)


def staged(duals, centroids):
    rows = centroids[0].shape[0]
    column = jax.ShapeDtypeStruct((rows, 1), jnp.float32)
    arrays = [jax.ShapeDtypeStruct(array.shape, array.dtype) for array in centroids]
    return pl.pallas_call(
        stage_kernel,
        in_specs=[VMEM] * 2 + [ANY] * 2,
        out_specs=[VMEM] * 4,
        out_shape=[column, column] + arrays,
        scratch_shapes=[pltpu.SemaphoreType.DMA],
        compiler_params=LIMIT,
    )(*[dual.reshape(rows // LANES, LANES) for dual in duals], *centroids)


def chunk_logits(factor, order, columns, centroids, pieces):
    rows, depth = centroids[0].shape
    devices = lax.axis_size(EVERY)
    f32 = jnp.float32
    logits = jax.ShapeDtypeStruct((4, rows, LANES), f32)
    block = pl.BlockSpec(logits.shape, lambda: (0, 0, 0))
    return pl.pallas_call(
        functools.partial(logits_kernel, factor),
        in_specs=[SMEM] + [VMEM] * (4 + len(pieces)),
        out_specs=[block, block, pl.BlockSpec((devices, 4, LANES), lambda: (0, 0, 0)), ANY],
        out_shape=[
            logits,
            logits,
            jax.ShapeDtypeStruct((devices, 4, LANES), f32),
            jax.ShapeDtypeStruct((4 * LANES, depth), pieces[0].dtype),
        ],
        scratch_shapes=[pltpu.VMEM((4, LANES), f32), pltpu.SemaphoreType.DMA],
        compiler_params=pltpu.CompilerParams(vmem_limit_bytes=24 * 2**20),
    )(order, *columns, *centroids, *[held(array) for array in pieces])


def send_rows(rows, out_ref):
    out_ref[...] = jnp.broadcast_to(rows.astype(out_ref.dtype)[None], out_ref.shape)


def first_kernel(order_ref, parts_ref, *refs):
    logits_refs = refs[:2]
    kernel_ref, passage_ref, centroid_ref, out_ref, sums_ref, sems = refs[2:]
    starts = (0, 4)
    copies = [
        pltpu.make_async_copy(ref, kernel_ref.at[pl.ds(start, ref.shape[0])], sems.at[number])
        for number, (ref, start) in enumerate(zip(logits_refs, starts))
    ]
    for copy in copies:
        copy.start()
    parts = parts_ref[...].reshape(parts_ref.shape[0] // 2, 2, 4, LANES)
    for core in range(2):
        part = parts[:, core]
        top = jnp.max(part, axis=0)
        passage_ref[core * 4 : core * 4 + 4, :] = -math.log(PASSAGES) - (
            top + jnp.log(jnp.sum(jnp.exp(part - top[None]), axis=0))
        )
    sums_ref[...] = to_local(order_ref, passage_ref[...])
    peak = None
    for k in range(CHUNKS):
        if k in starts:
            copies[starts.index(k)].wait()
        terms = kernel_ref[k] + sums_ref[pl.ds(order_ref[k], 1), :]
        kernel_ref[k] = terms
        peak = terms if peak is None else jnp.maximum(peak, terms)
    peak = jnp.max(peak, axis=1, keepdims=True)
    total = None
    for k in range(CHUNKS):
        terms = jnp.exp(kernel_ref[k] - peak)
        kernel_ref[k] = terms
        total = terms if total is None else total + terms
    total = jnp.sum(total, axis=1, keepdims=True)
    centroid_ref[...] = -math.log(CENTROIDS) - (peak + jnp.log(total))
    inverse = 1.0 / total
    for k in range(CHUNKS):
        terms = kernel_ref[k] * inverse
        kernel_ref[k] = terms
        sums_ref[pl.ds(order_ref[k], 1), :] = jnp.sum(terms, axis=0, keepdims=True)
    send_rows(to_common(order_ref, sums_ref[...]), out_ref)


def row_scale_of(parts_ref):
    parts = parts_ref[...].astype(jnp.float32)
    return (CENTROIDS / PASSAGES) / jnp.sum(parts, axis=0)


def column_sums(order_ref, kernel_ref, scale_ref):
    total = None
    for k in range(CHUNKS):
        terms = kernel_ref[k] * scale_ref[pl.ds(order_ref[k], 1), :]
        total = terms if total is None else total + terms
    return jnp.sum(total, axis=1, keepdims=True)


def middle_kernel(order_ref, parts_ref, kernel_ref, out_ref, sums_ref):
    sums_ref[...] = to_local(order_ref, row_scale_of(parts_ref))
    scale = 1.0 / column_sums(order_ref, kernel_ref, sums_ref)
    for k in range(CHUNKS):
        sums_ref[pl.ds(order_ref[k], 1), :] = jnp.sum(
            kernel_ref[k] * scale, axis=0, keepdims=True
        )
    send_rows(to_common(order_ref, sums_ref[...]), out_ref)


def last_kernel(order_ref, parts_ref, kernel_ref, passage_ref, centroid_ref, *refs):
    *piece_refs, new_ref, own_ref, duals_ref = refs[:-6]
    weight_ref, held_ref, tile_ref, scale_ref, sems, out_sems = refs[-6:]
    span, tiles = LANES, held_ref.shape[0]
    for tile in range(tiles):
        start = 0
        for ref in piece_refs:
            size = ref.shape[0]
            pltpu.make_async_copy(
                ref.at[:, pl.ds(tile * WIDTH, WIDTH)],
                held_ref.at[tile, pl.ds(start, size), :],
                sems.at[tile],
            ).start()
            start += size

    scale = row_scale_of(parts_ref)
    scale_ref[...] = to_local(order_ref, scale)
    total = column_sums(order_ref, kernel_ref, scale_ref)
    inverse = 1.0 / total
    for k in range(CHUNKS):
        weight_ref[:, k * span : (k + 1) * span] = (
            kernel_ref[k] * scale_ref[pl.ds(order_ref[k], 1), :] * inverse
        ).astype(weight_ref.dtype)

    def copy_out(tile):
        return pltpu.make_async_copy(
            tile_ref.at[tile % 2], new_ref.at[:, pl.ds(tile * WIDTH, WIDTH)], out_sems.at[tile % 2]
        )

    for tile in range(tiles):
        pltpu.make_async_copy(held_ref.at[tile], held_ref.at[tile], sems.at[tile]).wait()
        block = jnp.dot(
            weight_ref[...], held_ref[tile], preferred_element_type=jnp.float32
        ).astype(new_ref.dtype)
        if tile == 0:
            duals = centroid_ref[...] - jnp.log(total)
            square = (LANES, LANES)
            diagonal = lax.broadcasted_iota(jnp.int32, square, 0) == lax.broadcasted_iota(
                jnp.int32, square, 1
            )
            for k in range(duals.shape[0] // LANES):
                column = jnp.broadcast_to(duals[k * LANES : (k + 1) * LANES], square)
                duals_ref[pl.ds(k, 1), :] = jnp.sum(
                    jnp.where(diagonal, column, 0.0), axis=0, keepdims=True
                )
            scale_ref[...] = passage_ref[...] + jnp.log(scale)
            own = pltpu.roll(scale_ref[pl.ds(order_ref[CHUNKS], 1), :], LANES - order_ref[CHUNKS + 1], 1)
            own_ref[...] = own[:, : own_ref.shape[1]]
        if tile >= 2:
            copy_out(tile - 2).wait()
        tile_ref[tile % 2] = block
        copy_out(tile).start()
    for tile in range(tiles - 2, tiles):
        copy_out(tile).wait()


SMEM = pl.BlockSpec(memory_space=pltpu.SMEM)
VMEM = pl.BlockSpec(memory_space=pltpu.VMEM)
ANY = pl.BlockSpec(memory_space=pl.ANY)
LIMIT = pltpu.CompilerParams(vmem_limit_bytes=16 * 2**20)


def body(passages, centroids, dual_init):
    depth = passages.shape[1]
    local_rows = passages.shape[0]
    count = centroids.shape[0]
    factor = 4.0 / math.sqrt(depth)
    devices = lax.axis_size(EVERY)
    z, h, x, _, c = coords(lax.axis_index(EVERY))
    first = jnp.where(c == 0, x, z)
    second = jnp.where(c == 0, z, x)

    def fetch(step):
        def target(z, h, x, l, c):
            stays = h == c
            if stays and step == 0:
                return None
            h, l, c = (h, l, c) if stays else (1 - h, 1 - l, 1 - c)
            return (z, h, x - step, l, c) if c == 0 else (z - step, h, x, l, c)

        return move(passages, target)

    mine = jnp.where(h == c, passages, fetch(0))
    top = jnp.concatenate([mine, fetch(1)], axis=0)
    bottom = jnp.concatenate([fetch(2), fetch(3)], axis=0)
    bottom, near_duals = lax.optimization_barrier((bottom, to_sibling(dual_init)))
    top_before, bottom_after = along_second(top, 1), along_second(bottom, -1)
    bottom_before, top_after = along_second(bottom, 1), along_second(top, -1)
    top_across, bottom_across = along_second(top_before, 1), along_second(bottom_after, -1)
    arrived = [top, bottom, top_before, bottom_before, top_across, bottom_across, top_after, bottom_after]
    order = [c * 4 + (second + k) % 4 for k in OWN]
    order += [(1 - c) * 4 + (first + k) % 4 for k in OWN]
    row, lane = jnp.where(h == 0, z, 4 + x), jnp.where(h == 0, x, z) * local_rows
    order += [row, lane] + [x * local_rows, z * local_rows]
    order += [(4 - x) % 4 * local_rows, (4 - z) % 4 * local_rows]
    order = jnp.stack(order).astype(jnp.int32)

    pairs, _ = lax.optimization_barrier(
        ((dual_init, near_duals, centroids, to_sibling(centroids)), (top_before, bottom_after))
    )
    *columns, near, sibling = staged(pairs[:2], pairs[2:])
    arrived, near, sibling = lax.optimization_barrier((arrived, near, sibling))
    *logits, parts, arrived = chunk_logits(factor, order, columns, (near, sibling), arrived)
    logits = [logits[0], to_sibling(logits[1])]
    span = LANES
    f32 = jnp.float32
    parts = to_every(parts)
    pieces = [arrived, to_sibling(arrived)]

    sent = jax.ShapeDtypeStruct((devices, CHUNKS, span), jnp.bfloat16)
    block = pl.BlockSpec((devices, CHUNKS, span), lambda: (0, 0, 0))
    sums = pltpu.VMEM((CHUNKS, span), f32)
    kernel, passage_first, centroid_first, partial = pl.pallas_call(
        first_kernel,
        in_specs=[SMEM, VMEM] + [ANY] * len(logits),
        out_specs=[VMEM] * 3 + [block],
        out_shape=[
            jax.ShapeDtypeStruct((CHUNKS, count, span), f32),
            jax.ShapeDtypeStruct((CHUNKS, span), f32),
            jax.ShapeDtypeStruct((count, 1), f32),
            sent,
        ],
        scratch_shapes=[sums, pltpu.SemaphoreType.DMA((len(logits),))],
        compiler_params=LIMIT,
    )(order, parts, *logits)
    partial, *pieces = lax.optimization_barrier((partial, *pieces))
    partial = pl.pallas_call(
        middle_kernel,
        in_specs=[SMEM, VMEM, VMEM],
        out_specs=block,
        out_shape=sent,
        scratch_shapes=[sums],
        compiler_params=LIMIT,
    )(order, to_every(partial), kernel)
    new_centroids, own_duals, centroid_duals = pl.pallas_call(
        last_kernel,
        in_specs=[SMEM] + [VMEM] * 4 + [ANY] * len(pieces),
        out_specs=[ANY, VMEM, VMEM],
        out_shape=[
            jax.ShapeDtypeStruct((count, depth), jnp.bfloat16),
            jax.ShapeDtypeStruct((1, local_rows), f32),
            jax.ShapeDtypeStruct((count // LANES, LANES), f32),
        ],
        scratch_shapes=[
            pltpu.VMEM((count, CHUNKS * span), jnp.bfloat16),
            pltpu.VMEM((depth // WIDTH, CHUNKS * span, WIDTH), jnp.bfloat16),
            pltpu.VMEM((2, count, WIDTH), jnp.bfloat16),
            sums,
            pltpu.SemaphoreType.DMA((depth // WIDTH,)),
            pltpu.SemaphoreType.DMA((2,)),
        ],
        compiler_params=pltpu.CompilerParams(vmem_limit_bytes=24 * 2**20),
    )(order, to_every(partial), kernel, passage_first, centroid_first, *pieces)
    own_duals = own_duals.reshape(local_rows)
    return (new_centroids, own_duals, centroid_duals.reshape(count))


def solution(mesh):
    in_specs = (P("psg", None), P(("psg", "cen"), None), P(("psg", "cen")))
    out_specs = (P(("psg", "cen"), None), P("psg"), P(("psg", "cen")))
    return jax.shard_map(body, mesh=mesh, in_specs=in_specs, out_specs=out_specs, check_vma=False)
```

```python
import functools
import math

import jax
import jax.numpy as jnp
from jax import lax
from jax.experimental import pallas as pl
from jax.experimental.pallas import tpu as pltpu
from jax.sharding import PartitionSpec as P

CENTROIDS = 65536
PASSAGES = 1024
EVERY = ("psg", "cen")
X, Z, HALVES = 4, 4, 2
CHUNKS = 8
OWN = (0, 3, 1, 2)
LANES = 128
WIDTH = 2048
PARTS = 16


def coords(device):
    return (
        device // (HALVES * X * 4),
        device // (X * 4) % HALVES,
        device // 4 % X,
        device // 2 % 2,
        device % 2,
    )


def move(value, target):
    pairs = []
    for device in range(Z * HALVES * X * 4):
        there = target(*coords(device))
        if there is not None:
            z, h, x, l, c = there
            pairs.append((device, (((z % Z) * HALVES + h) * X + x % X) * 4 + l * 2 + c))
    return lax.ppermute(value, EVERY, pairs)


def along_second(value, step):
    return move(
        value,
        lambda z, h, x, l, c: (z + step, h, x, l, c) if c == 0 else (z, h, x + step, l, c),
    )


def to_sibling(value):
    return move(value, lambda z, h, x, l, c: (z, h, x, l, 1 - c))


def to_every(copies):
    return lax.all_to_all(copies, EVERY, 0, 0)


def rolled(order_ref, first, rows):
    low = lax.broadcasted_iota(jnp.int32, rows.shape, 0) < 4
    return jnp.where(
        low, pltpu.roll(rows, order_ref[first], 1), pltpu.roll(rows, order_ref[first + 1], 1)
    )


def to_common(order_ref, rows):
    return rolled(order_ref, CHUNKS + 2, rows)


def to_local(order_ref, rows):
    return rolled(order_ref, CHUNKS + 4, rows)


def mixed(rows_ref, one, two):
    low = lax.broadcasted_iota(jnp.int32, (1, LANES), 1) < LANES // 2
    a, b = rows_ref[pl.ds(one, 1), :], rows_ref[pl.ds(two, 1), :]
    rows_ref[pl.ds(one, 1), :] = jnp.where(low, a, b)
    rows_ref[pl.ds(two, 1), :] = jnp.where(low, b, a)


def both_mixed(order_ref, rows_ref):
    for slot in (0, 4):
        mixed(rows_ref, order_ref[slot + 1], order_ref[slot + 2])


def two_chunks(factor, columns_refs, centroids_refs, piece_refs, logits_refs, ready):
    chunks = jnp.concatenate([ref[...] for ref in piece_refs], axis=0)
    tops, totals = [], []
    for number in range(2):
        ready(number)
        product = factor * lax.dot_general(
            centroids_refs[number][...],
            chunks,
            (((1,), (1,)), ((), ())),
            preferred_element_type=jnp.float32,
        )
        for k in range(2):
            logits_refs[number][k] = product[:, k * LANES : (k + 1) * LANES]
        shifted = product + columns_refs[number][...]
        top = jnp.max(shifted, axis=0, keepdims=True)
        tops.append(top)
        totals.append(jnp.sum(jnp.exp(shifted - top), axis=0, keepdims=True))
    top = jnp.maximum(*tops)
    logsum = top + jnp.log(sum(total * jnp.exp(own - top) for own, total in zip(tops, totals)))
    return [logsum[:, k * LANES : (k + 1) * LANES] for k in range(2)]


def gathered(piece_refs, arrived_ref, sem):
    start = 0
    for ref in piece_refs:
        size = ref.shape[0]
        pltpu.make_async_copy(ref, arrived_ref.at[pl.ds(start, size)], sem).start()
        start += size


def early_kernel(factor, *refs):
    rows_refs, centroids_refs, piece_refs = refs[:2], refs[2:4], refs[4:8]
    columns_refs, held_refs, logits_refs, logsum_ref, arrived_ref = refs[8:10], refs[10:12], refs[12:14], refs[14], refs[15]
    sems, sem = refs[16:]
    for number in range(2):
        size = held_refs[number].shape[0] // PARTS
        for part in range(PARTS):
            rows = pl.ds(part * size, size)
            pltpu.make_async_copy(
                centroids_refs[number].at[rows], held_refs[number].at[rows], sems.at[number]
            ).start()
    gathered(piece_refs, arrived_ref, sem)
    square = (LANES, LANES)
    diagonal = lax.broadcasted_iota(jnp.int32, square, 0) == lax.broadcasted_iota(
        jnp.int32, square, 1
    )
    for source, target in zip(rows_refs, columns_refs):
        for k in range(source.shape[0]):
            row = jnp.broadcast_to(source[k : k + 1, :], square)
            target[k * LANES : (k + 1) * LANES, :] = jnp.sum(
                jnp.where(diagonal, row, 0.0), axis=1, keepdims=True
            )

    def ready(number):
        pltpu.make_async_copy(held_refs[number], held_refs[number], sems.at[number]).wait()

    logsums = two_chunks(factor, columns_refs, held_refs, piece_refs, logits_refs, ready)
    for k in range(2):
        logsum_ref[k : k + 1, :] = logsums[k]
    pltpu.make_async_copy(arrived_ref, arrived_ref, sem).wait()


def late_kernel(factor, order_ref, *refs):
    columns_refs, centroids_refs, piece_refs, earlier_ref = refs[:2], refs[2:4], refs[4:8], refs[8]
    logits_refs, out_ref, arrived_ref, rows_ref, sem = refs[9:11], refs[11], refs[12], refs[13], refs[14]
    gathered(piece_refs, arrived_ref, sem)
    logsums = [earlier_ref[k : k + 1, :] for k in range(2)]
    logsums += two_chunks(
        factor, columns_refs, centroids_refs, piece_refs, logits_refs, lambda number: None
    )
    for k in range(4):
        rows_ref[pl.ds(lax.rem(order_ref[k], 4), 1), :] = logsums[k]
    mixed(rows_ref, lax.rem(order_ref[1], 4), lax.rem(order_ref[2], 4))
    core = lax.div(order_ref[0], 4)
    send_rows(pltpu.roll(rows_ref[...], order_ref[CHUNKS + 2 + core], 1), out_ref)
    pltpu.make_async_copy(arrived_ref, arrived_ref, sem).wait()


def held(array):
    return pltpu.with_memory_space_constraint(array, pltpu.VMEM)


def early_logits(factor, duals, centroids, pieces):
    rows, depth = centroids[0].shape
    f32 = jnp.float32
    column = jax.ShapeDtypeStruct((rows, 1), f32)
    logits = jax.ShapeDtypeStruct((2, rows, LANES), f32)
    block = pl.BlockSpec(logits.shape, lambda: (0, 0, 0))
    return pl.pallas_call(
        functools.partial(early_kernel, factor),
        in_specs=[VMEM] * 2 + [ANY] * 2 + [VMEM] * len(pieces),
        out_specs=[VMEM] * 4 + [block, block, VMEM, ANY],
        out_shape=[column, column]
        + [jax.ShapeDtypeStruct(array.shape, array.dtype) for array in centroids]
        + [logits, logits]
        + [
            jax.ShapeDtypeStruct((2, LANES), f32),
            jax.ShapeDtypeStruct((2 * LANES, depth), pieces[0].dtype),
        ],
        scratch_shapes=[pltpu.SemaphoreType.DMA((2,)), pltpu.SemaphoreType.DMA],
        compiler_params=pltpu.CompilerParams(vmem_limit_bytes=24 * 2**20),
    )(*[dual.reshape(rows // LANES, LANES) for dual in duals], *centroids, *map(held, pieces))


def late_logits(factor, order, columns, centroids, pieces, earlier):
    rows, depth = centroids[0].shape
    devices = lax.axis_size(EVERY)
    f32 = jnp.float32
    logits = jax.ShapeDtypeStruct((2, rows, LANES), f32)
    block = pl.BlockSpec(logits.shape, lambda: (0, 0, 0))
    return pl.pallas_call(
        functools.partial(late_kernel, factor),
        in_specs=[SMEM] + [VMEM] * (5 + len(pieces)),
        out_specs=[block, block, pl.BlockSpec((devices, 4, LANES), lambda: (0, 0, 0)), ANY],
        out_shape=[
            logits,
            logits,
            jax.ShapeDtypeStruct((devices, 4, LANES), f32),
            jax.ShapeDtypeStruct((2 * LANES, depth), pieces[0].dtype),
        ],
        scratch_shapes=[pltpu.VMEM((4, LANES), f32), pltpu.SemaphoreType.DMA],
        compiler_params=pltpu.CompilerParams(vmem_limit_bytes=24 * 2**20),
    )(order, *columns, *centroids, *map(held, pieces), earlier)


def send_rows(rows, out_ref):
    out_ref[...] = jnp.broadcast_to(rows.astype(out_ref.dtype)[None], out_ref.shape)


def first_kernel(order_ref, parts_ref, *refs):
    logits_refs = refs[:4]
    kernel_ref, passage_ref, centroid_ref, out_ref, sums_ref, sems = refs[4:]
    starts = (0, 2, 4, 6)
    copies = [
        pltpu.make_async_copy(ref, kernel_ref.at[pl.ds(start, ref.shape[0])], sems.at[number])
        for number, (ref, start) in enumerate(zip(logits_refs, starts))
    ]
    for copy in copies:
        copy.start()
    parts = parts_ref[...].reshape(parts_ref.shape[0] // 2, 2, 4, LANES)
    for core in range(2):
        part = parts[:, core]
        top = jnp.max(part, axis=0)
        passage_ref[core * 4 : core * 4 + 4, :] = -math.log(PASSAGES) - (
            top + jnp.log(jnp.sum(jnp.exp(part - top[None]), axis=0))
        )
    sums_ref[...] = to_local(order_ref, passage_ref[...])
    both_mixed(order_ref, sums_ref)
    peak = None
    for k in range(CHUNKS):
        if k in starts:
            copies[starts.index(k)].wait()
        terms = kernel_ref[k] + sums_ref[pl.ds(order_ref[k], 1), :]
        kernel_ref[k] = terms
        peak = terms if peak is None else jnp.maximum(peak, terms)
    peak = jnp.max(peak, axis=1, keepdims=True)
    total = None
    for k in range(CHUNKS):
        terms = jnp.exp(kernel_ref[k] - peak)
        kernel_ref[k] = terms
        total = terms if total is None else total + terms
    total = jnp.sum(total, axis=1, keepdims=True)
    centroid_ref[...] = -math.log(CENTROIDS) - (peak + jnp.log(total))
    inverse = 1.0 / total
    for k in range(CHUNKS):
        terms = kernel_ref[k] * inverse
        kernel_ref[k] = terms
        sums_ref[pl.ds(order_ref[k], 1), :] = jnp.sum(terms, axis=0, keepdims=True)
    both_mixed(order_ref, sums_ref)
    send_rows(to_common(order_ref, sums_ref[...]), out_ref)


def row_scale_of(parts_ref):
    parts = parts_ref[...].astype(jnp.float32)
    return (CENTROIDS / PASSAGES) / jnp.sum(parts, axis=0)


def column_sums(order_ref, kernel_ref, scale_ref):
    total = None
    for k in range(CHUNKS):
        terms = kernel_ref[k] * scale_ref[pl.ds(order_ref[k], 1), :]
        total = terms if total is None else total + terms
    return jnp.sum(total, axis=1, keepdims=True)


def middle_kernel(order_ref, parts_ref, kernel_ref, out_ref, sums_ref):
    sums_ref[...] = to_local(order_ref, row_scale_of(parts_ref))
    both_mixed(order_ref, sums_ref)
    scale = 1.0 / column_sums(order_ref, kernel_ref, sums_ref)
    for k in range(CHUNKS):
        sums_ref[pl.ds(order_ref[k], 1), :] = jnp.sum(
            kernel_ref[k] * scale, axis=0, keepdims=True
        )
    both_mixed(order_ref, sums_ref)
    send_rows(to_common(order_ref, sums_ref[...]), out_ref)


def last_kernel(order_ref, parts_ref, kernel_ref, passage_ref, centroid_ref, *refs):
    *piece_refs, new_ref, own_ref, duals_ref = refs[:-6]
    weight_ref, held_ref, tile_ref, scale_ref, sems, out_sems = refs[-6:]
    span, tiles = LANES, held_ref.shape[0]
    for tile in range(tiles):
        start = 0
        for ref in piece_refs:
            size = ref.shape[0]
            pltpu.make_async_copy(
                ref.at[:, pl.ds(tile * WIDTH, WIDTH)],
                held_ref.at[tile, pl.ds(start, size), :],
                sems.at[tile],
            ).start()
            start += size

    scale = row_scale_of(parts_ref)
    scale_ref[...] = to_local(order_ref, scale)
    both_mixed(order_ref, scale_ref)
    total = column_sums(order_ref, kernel_ref, scale_ref)
    inverse = 1.0 / total
    for k in range(CHUNKS):
        weight_ref[:, k * span : (k + 1) * span] = (
            kernel_ref[k] * scale_ref[pl.ds(order_ref[k], 1), :] * inverse
        ).astype(weight_ref.dtype)

    def copy_out(tile):
        return pltpu.make_async_copy(
            tile_ref.at[tile % 2], new_ref.at[:, pl.ds(tile * WIDTH, WIDTH)], out_sems.at[tile % 2]
        )

    for tile in range(tiles):
        pltpu.make_async_copy(held_ref.at[tile], held_ref.at[tile], sems.at[tile]).wait()
        block = jnp.dot(
            weight_ref[...], held_ref[tile], preferred_element_type=jnp.float32
        ).astype(new_ref.dtype)
        if tile == 0:
            duals = centroid_ref[...] - jnp.log(total)
            square = (LANES, LANES)
            diagonal = lax.broadcasted_iota(jnp.int32, square, 0) == lax.broadcasted_iota(
                jnp.int32, square, 1
            )
            for k in range(duals.shape[0] // LANES):
                column = jnp.broadcast_to(duals[k * LANES : (k + 1) * LANES], square)
                duals_ref[pl.ds(k, 1), :] = jnp.sum(
                    jnp.where(diagonal, column, 0.0), axis=0, keepdims=True
                )
            scale_ref[...] = passage_ref[...] + jnp.log(scale)
            own = pltpu.roll(scale_ref[pl.ds(order_ref[CHUNKS], 1), :], LANES - order_ref[CHUNKS + 1], 1)
            own_ref[...] = own[:, : own_ref.shape[1]]
        if tile >= 2:
            copy_out(tile - 2).wait()
        tile_ref[tile % 2] = block
        copy_out(tile).start()
    for tile in range(tiles - 2, tiles):
        copy_out(tile).wait()


SMEM = pl.BlockSpec(memory_space=pltpu.SMEM)
VMEM = pl.BlockSpec(memory_space=pltpu.VMEM)
ANY = pl.BlockSpec(memory_space=pl.ANY)
LIMIT = pltpu.CompilerParams(vmem_limit_bytes=16 * 2**20)


def body(passages, centroids, dual_init):
    depth = passages.shape[1]
    local_rows = passages.shape[0]
    count = centroids.shape[0]
    factor = 4.0 / math.sqrt(depth)
    devices = lax.axis_size(EVERY)
    z, h, x, _, c = coords(lax.axis_index(EVERY))
    first = jnp.where(c == 0, x, z)
    second = jnp.where(c == 0, z, x)

    def fetch(step):
        def target(z, h, x, l, c):
            stays = h == c
            if stays and step == 0:
                return None
            h, l, c = (h, l, c) if stays else (1 - h, 1 - l, 1 - c)
            return (z, h, x - step, l, c) if c == 0 else (z - step, h, x, l, c)

        return move(passages, target)

    mine = jnp.where(h == c, passages, fetch(0))
    top = jnp.concatenate([mine, fetch(1)], axis=0)
    bottom = jnp.concatenate([fetch(2), fetch(3)], axis=0)
    bottom, near_duals = lax.optimization_barrier((bottom, to_sibling(dual_init)))
    top_before, bottom_after = along_second(top, 1), along_second(bottom, -1)
    bottom_before, top_after = along_second(bottom, 1), along_second(top, -1)
    top_across, bottom_across = along_second(top_before, 1), along_second(bottom_after, -1)
    first_pieces = [top, bottom, top_before, bottom_after]
    last_pieces = [top_after, bottom_before, top_across, bottom_across]
    order = [c * 4 + (second + k) % 4 for k in OWN]
    order += [(1 - c) * 4 + (first + k) % 4 for k in OWN]
    row, lane = jnp.where(h == 0, z, 4 + x), jnp.where(h == 0, x, z) * local_rows
    order += [row, lane] + [x * local_rows, z * local_rows]
    order += [(4 - x) % 4 * local_rows, (4 - z) % 4 * local_rows]
    order = jnp.stack(order).astype(jnp.int32)

    pairs, first_pieces = lax.optimization_barrier(
        ((dual_init, near_duals, centroids, to_sibling(centroids)), first_pieces)
    )
    early = early_logits(factor, pairs[:2], pairs[2:], first_pieces)
    last_pieces, early = lax.optimization_barrier((last_pieces, early))
    late = late_logits(factor, order, early[:2], early[2:4], last_pieces, early[6])
    logits = [early[4], late[0], to_sibling(early[5]), to_sibling(late[1])]
    parts, arrived = late[2], [early[7], late[3]]
    span = LANES
    f32 = jnp.float32
    parts = to_every(parts)
    pieces = arrived + [to_sibling(array) for array in arrived]

    sent = jax.ShapeDtypeStruct((devices, CHUNKS, span), jnp.bfloat16)
    block = pl.BlockSpec((devices, CHUNKS, span), lambda: (0, 0, 0))
    sums = pltpu.VMEM((CHUNKS, span), f32)
    kernel, passage_first, centroid_first, partial = pl.pallas_call(
        first_kernel,
        in_specs=[SMEM, VMEM] + [ANY] * len(logits),
        out_specs=[VMEM] * 3 + [block],
        out_shape=[
            jax.ShapeDtypeStruct((CHUNKS, count, span), f32),
            jax.ShapeDtypeStruct((CHUNKS, span), f32),
            jax.ShapeDtypeStruct((count, 1), f32),
            sent,
        ],
        scratch_shapes=[sums, pltpu.SemaphoreType.DMA((len(logits),))],
        compiler_params=LIMIT,
    )(order, parts, *logits)
    partial, *pieces = lax.optimization_barrier((partial, *pieces))
    partial = pl.pallas_call(
        middle_kernel,
        in_specs=[SMEM, VMEM, VMEM],
        out_specs=block,
        out_shape=sent,
        scratch_shapes=[sums],
        compiler_params=LIMIT,
    )(order, to_every(partial), kernel)
    new_centroids, own_duals, centroid_duals = pl.pallas_call(
        last_kernel,
        in_specs=[SMEM] + [VMEM] * 4 + [ANY] * len(pieces),
        out_specs=[ANY, VMEM, VMEM],
        out_shape=[
            jax.ShapeDtypeStruct((count, depth), jnp.bfloat16),
            jax.ShapeDtypeStruct((1, local_rows), f32),
            jax.ShapeDtypeStruct((count // LANES, LANES), f32),
        ],
        scratch_shapes=[
            pltpu.VMEM((count, CHUNKS * span), jnp.bfloat16),
            pltpu.VMEM((depth // WIDTH, CHUNKS * span, WIDTH), jnp.bfloat16),
            pltpu.VMEM((2, count, WIDTH), jnp.bfloat16),
            sums,
            pltpu.SemaphoreType.DMA((depth // WIDTH,)),
            pltpu.SemaphoreType.DMA((2,)),
        ],
        compiler_params=pltpu.CompilerParams(vmem_limit_bytes=24 * 2**20),
    )(order, to_every(partial), kernel, passage_first, centroid_first, *pieces)
    own_duals = own_duals.reshape(local_rows)
    return (new_centroids, own_duals, centroid_duals.reshape(count))


def solution(mesh):
    in_specs = (P("psg", None), P(("psg", "cen"), None), P(("psg", "cen")))
    out_specs = (P(("psg", "cen"), None), P("psg"), P(("psg", "cen")))
    return jax.shard_map(body, mesh=mesh, in_specs=in_specs, out_specs=out_specs, check_vma=False)
```

```python
import functools
import math

import jax
import jax.numpy as jnp
from jax import lax
from jax.experimental import pallas as pl
from jax.experimental.pallas import tpu as pltpu
from jax.sharding import PartitionSpec as P

CENTROIDS = 65536
PASSAGES = 1024
EVERY = ("psg", "cen")
X, Z, HALVES = 4, 4, 2
CHUNKS = 8
OWN = (0, 3, 1, 2)
LANES = 128
WIDTH = 2048
PARTS = 16


def coords(device):
    return (
        device // (HALVES * X * 4),
        device // (X * 4) % HALVES,
        device // 4 % X,
        device // 2 % 2,
        device % 2,
    )


def move(value, target):
    pairs = []
    for device in range(Z * HALVES * X * 4):
        there = target(*coords(device))
        if there is not None:
            z, h, x, l, c = there
            pairs.append((device, (((z % Z) * HALVES + h) * X + x % X) * 4 + l * 2 + c))
    return lax.ppermute(value, EVERY, pairs)


def along_second(value, step):
    return move(
        value,
        lambda z, h, x, l, c: (z + step, h, x, l, c) if c == 0 else (z, h, x + step, l, c),
    )


def to_sibling(value):
    return move(value, lambda z, h, x, l, c: (z, h, x, l, 1 - c))


def to_every(copies):
    return lax.all_to_all(copies, EVERY, 0, 0)


def rolled(order_ref, first, rows):
    low = lax.broadcasted_iota(jnp.int32, rows.shape, 0) < 4
    return jnp.where(
        low, pltpu.roll(rows, order_ref[first], 1), pltpu.roll(rows, order_ref[first + 1], 1)
    )


def to_common(order_ref, rows):
    return rolled(order_ref, CHUNKS + 2, rows)


def to_local(order_ref, rows):
    return rolled(order_ref, CHUNKS + 4, rows)


def mixed(rows_ref, one, two):
    low = lax.broadcasted_iota(jnp.int32, (1, LANES), 1) < LANES // 2
    a, b = rows_ref[pl.ds(one, 1), :], rows_ref[pl.ds(two, 1), :]
    rows_ref[pl.ds(one, 1), :] = jnp.where(low, a, b)
    rows_ref[pl.ds(two, 1), :] = jnp.where(low, b, a)


def both_mixed(order_ref, rows_ref):
    for slot in (0, 4):
        mixed(rows_ref, order_ref[slot + 1], order_ref[slot + 2])


def two_chunks(factor, columns_refs, centroids_refs, piece_refs, logits_refs, ready):
    chunks = jnp.concatenate([ref[...] for ref in piece_refs], axis=0)
    tops, totals = [], []
    for number in range(2):
        ready(number)
        product = factor * lax.dot_general(
            centroids_refs[number][...],
            chunks,
            (((1,), (1,)), ((), ())),
            preferred_element_type=jnp.float32,
        )
        for k in range(2):
            logits_refs[number][k] = product[:, k * LANES : (k + 1) * LANES]
        shifted = product + columns_refs[number][...]
        top = jnp.max(shifted, axis=0, keepdims=True)
        tops.append(top)
        totals.append(jnp.sum(jnp.exp(shifted - top), axis=0, keepdims=True))
    top = jnp.maximum(*tops)
    logsum = top + jnp.log(sum(total * jnp.exp(own - top) for own, total in zip(tops, totals)))
    return [logsum[:, k * LANES : (k + 1) * LANES] for k in range(2)]


def gathered(piece_refs, arrived_ref, sem):
    start = 0
    for ref in piece_refs:
        size = ref.shape[0]
        pltpu.make_async_copy(ref, arrived_ref.at[pl.ds(start, size)], sem).start()
        start += size


def early_kernel(factor, *refs):
    rows_refs, centroids_refs, piece_refs = refs[:2], refs[2:4], refs[4:8]
    columns_refs, held_refs, logits_refs, logsum_ref = refs[8:10], refs[10:12], refs[12:14], refs[14]
    arrived_ref = refs[15].at[pl.ds(0, 2 * LANES)]
    sems, sem = refs[16:]
    for number in range(2):
        size = held_refs[number].shape[0] // PARTS
        for part in range(PARTS):
            rows = pl.ds(part * size, size)
            pltpu.make_async_copy(
                centroids_refs[number].at[rows], held_refs[number].at[rows], sems.at[number]
            ).start()
    gathered(piece_refs, arrived_ref, sem)
    square = (LANES, LANES)
    diagonal = lax.broadcasted_iota(jnp.int32, square, 0) == lax.broadcasted_iota(
        jnp.int32, square, 1
    )
    for source, target in zip(rows_refs, columns_refs):
        for k in range(source.shape[0]):
            row = jnp.broadcast_to(source[k : k + 1, :], square)
            target[k * LANES : (k + 1) * LANES, :] = jnp.sum(
                jnp.where(diagonal, row, 0.0), axis=1, keepdims=True
            )

    def ready(number):
        pltpu.make_async_copy(held_refs[number], held_refs[number], sems.at[number]).wait()

    logsums = two_chunks(factor, columns_refs, held_refs, piece_refs, logits_refs, ready)
    for k in range(2):
        logsum_ref[k : k + 1, :] = logsums[k]
    pltpu.make_async_copy(arrived_ref, arrived_ref, sem).wait()


def late_kernel(factor, order_ref, *refs):
    columns_refs, centroids_refs, piece_refs, earlier_ref = refs[:2], refs[2:4], refs[4:8], refs[8]
    logits_refs, out_ref, all_ref, rows_ref, sem = refs[10:12], refs[12], refs[13], refs[14], refs[15]
    arrived_ref = all_ref.at[pl.ds(2 * LANES, 2 * LANES)]
    gathered(piece_refs, arrived_ref, sem)
    logsums = [earlier_ref[k : k + 1, :] for k in range(2)]
    logsums += two_chunks(
        factor, columns_refs, centroids_refs, piece_refs, logits_refs, lambda number: None
    )
    for k in range(4):
        rows_ref[pl.ds(lax.rem(order_ref[k], 4), 1), :] = logsums[k]
    mixed(rows_ref, lax.rem(order_ref[1], 4), lax.rem(order_ref[2], 4))
    core = lax.div(order_ref[0], 4)
    send_rows(pltpu.roll(rows_ref[...], order_ref[CHUNKS + 2 + core], 1), out_ref)
    pltpu.make_async_copy(arrived_ref, arrived_ref, sem).wait()


def held(array):
    return pltpu.with_memory_space_constraint(array, pltpu.VMEM)


def early_logits(factor, duals, centroids, pieces):
    rows, depth = centroids[0].shape
    f32 = jnp.float32
    column = jax.ShapeDtypeStruct((rows, 1), f32)
    logits = jax.ShapeDtypeStruct((2, rows, LANES), f32)
    block = pl.BlockSpec(logits.shape, lambda: (0, 0, 0))
    return pl.pallas_call(
        functools.partial(early_kernel, factor),
        in_specs=[VMEM] * 2 + [ANY] * 2 + [VMEM] * len(pieces),
        out_specs=[VMEM] * 4 + [block, block, VMEM, ANY],
        out_shape=[column, column]
        + [jax.ShapeDtypeStruct(array.shape, array.dtype) for array in centroids]
        + [logits, logits]
        + [
            jax.ShapeDtypeStruct((2, LANES), f32),
            jax.ShapeDtypeStruct((4 * LANES, depth), pieces[0].dtype),
        ],
        scratch_shapes=[pltpu.SemaphoreType.DMA((2,)), pltpu.SemaphoreType.DMA],
        compiler_params=pltpu.CompilerParams(vmem_limit_bytes=24 * 2**20),
    )(*[dual.reshape(rows // LANES, LANES) for dual in duals], *centroids, *map(held, pieces))


def late_logits(factor, order, columns, centroids, pieces, earlier, arrived):
    rows, depth = centroids[0].shape
    devices = lax.axis_size(EVERY)
    f32 = jnp.float32
    logits = jax.ShapeDtypeStruct((2, rows, LANES), f32)
    block = pl.BlockSpec(logits.shape, lambda: (0, 0, 0))
    return pl.pallas_call(
        functools.partial(late_kernel, factor),
        in_specs=[SMEM] + [VMEM] * (5 + len(pieces)) + [ANY],
        out_specs=[block, block, pl.BlockSpec((devices, 4, LANES), lambda: (0, 0, 0)), ANY],
        out_shape=[
            logits,
            logits,
            jax.ShapeDtypeStruct((devices, 4, LANES), f32),
            jax.ShapeDtypeStruct((4 * LANES, depth), pieces[0].dtype),
        ],
        scratch_shapes=[pltpu.VMEM((4, LANES), f32), pltpu.SemaphoreType.DMA],
        compiler_params=pltpu.CompilerParams(vmem_limit_bytes=24 * 2**20),
        input_output_aliases={10: 3},
    )(order, *columns, *centroids, *map(held, pieces), earlier, arrived)


def send_rows(rows, out_ref):
    out_ref[...] = jnp.broadcast_to(rows.astype(out_ref.dtype)[None], out_ref.shape)


def first_kernel(order_ref, parts_ref, *refs):
    logits_refs = refs[:4]
    kernel_ref, passage_ref, centroid_ref, out_ref, sums_ref, sems = refs[4:]
    starts = (0, 2, 4, 6)
    copies = [
        pltpu.make_async_copy(ref, kernel_ref.at[pl.ds(start, ref.shape[0])], sems.at[number])
        for number, (ref, start) in enumerate(zip(logits_refs, starts))
    ]
    for copy in copies:
        copy.start()
    parts = parts_ref[...].reshape(parts_ref.shape[0] // 2, 2, 4, LANES)
    for core in range(2):
        part = parts[:, core]
        top = jnp.max(part, axis=0)
        passage_ref[core * 4 : core * 4 + 4, :] = -math.log(PASSAGES) - (
            top + jnp.log(jnp.sum(jnp.exp(part - top[None]), axis=0))
        )
    sums_ref[...] = to_local(order_ref, passage_ref[...])
    both_mixed(order_ref, sums_ref)
    peak = None
    for k in range(CHUNKS):
        if k in starts:
            copies[starts.index(k)].wait()
        terms = kernel_ref[k] + sums_ref[pl.ds(order_ref[k], 1), :]
        kernel_ref[k] = terms
        peak = terms if peak is None else jnp.maximum(peak, terms)
    peak = jnp.max(peak, axis=1, keepdims=True)
    total = None
    for k in range(CHUNKS):
        terms = jnp.exp(kernel_ref[k] - peak)
        kernel_ref[k] = terms
        total = terms if total is None else total + terms
    total = jnp.sum(total, axis=1, keepdims=True)
    centroid_ref[...] = -math.log(CENTROIDS) - (peak + jnp.log(total))
    inverse = 1.0 / total
    for k in range(CHUNKS):
        terms = kernel_ref[k] * inverse
        kernel_ref[k] = terms
        sums_ref[pl.ds(order_ref[k], 1), :] = jnp.sum(terms, axis=0, keepdims=True)
    both_mixed(order_ref, sums_ref)
    send_rows(to_common(order_ref, sums_ref[...]), out_ref)


def row_scale_of(parts_ref):
    parts = parts_ref[...].astype(jnp.float32)
    return (CENTROIDS / PASSAGES) / jnp.sum(parts, axis=0)


def column_sums(order_ref, kernel_ref, scale_ref):
    total = None
    for k in range(CHUNKS):
        terms = kernel_ref[k] * scale_ref[pl.ds(order_ref[k], 1), :]
        total = terms if total is None else total + terms
    return jnp.sum(total, axis=1, keepdims=True)


def middle_kernel(order_ref, parts_ref, kernel_ref, out_ref, sums_ref):
    sums_ref[...] = to_local(order_ref, row_scale_of(parts_ref))
    both_mixed(order_ref, sums_ref)
    scale = 1.0 / column_sums(order_ref, kernel_ref, sums_ref)
    for k in range(CHUNKS):
        sums_ref[pl.ds(order_ref[k], 1), :] = jnp.sum(
            kernel_ref[k] * scale, axis=0, keepdims=True
        )
    both_mixed(order_ref, sums_ref)
    send_rows(to_common(order_ref, sums_ref[...]), out_ref)


def last_kernel(order_ref, parts_ref, kernel_ref, passage_ref, centroid_ref, *refs):
    *piece_refs, new_ref, own_ref, duals_ref = refs[:-6]
    weight_ref, held_ref, tile_ref, scale_ref, sems, out_sems = refs[-6:]
    span, tiles = LANES, held_ref.shape[0]
    for tile in range(tiles):
        start = 0
        for ref in piece_refs:
            size = ref.shape[0]
            pltpu.make_async_copy(
                ref.at[:, pl.ds(tile * WIDTH, WIDTH)],
                held_ref.at[tile, pl.ds(start, size), :],
                sems.at[tile],
            ).start()
            start += size

    scale = row_scale_of(parts_ref)
    scale_ref[...] = to_local(order_ref, scale)
    both_mixed(order_ref, scale_ref)
    total = column_sums(order_ref, kernel_ref, scale_ref)
    inverse = 1.0 / total
    for k in range(CHUNKS):
        weight_ref[:, k * span : (k + 1) * span] = (
            kernel_ref[k] * scale_ref[pl.ds(order_ref[k], 1), :] * inverse
        ).astype(weight_ref.dtype)

    def copy_out(tile):
        return pltpu.make_async_copy(
            tile_ref.at[tile % 2], new_ref.at[:, pl.ds(tile * WIDTH, WIDTH)], out_sems.at[tile % 2]
        )

    for tile in range(tiles):
        pltpu.make_async_copy(held_ref.at[tile], held_ref.at[tile], sems.at[tile]).wait()
        block = jnp.dot(
            weight_ref[...], held_ref[tile], preferred_element_type=jnp.float32
        ).astype(new_ref.dtype)
        if tile == 0:
            duals = centroid_ref[...] - jnp.log(total)
            square = (LANES, LANES)
            diagonal = lax.broadcasted_iota(jnp.int32, square, 0) == lax.broadcasted_iota(
                jnp.int32, square, 1
            )
            for k in range(duals.shape[0] // LANES):
                column = jnp.broadcast_to(duals[k * LANES : (k + 1) * LANES], square)
                duals_ref[pl.ds(k, 1), :] = jnp.sum(
                    jnp.where(diagonal, column, 0.0), axis=0, keepdims=True
                )
            scale_ref[...] = passage_ref[...] + jnp.log(scale)
            own = pltpu.roll(scale_ref[pl.ds(order_ref[CHUNKS], 1), :], LANES - order_ref[CHUNKS + 1], 1)
            own_ref[...] = own[:, : own_ref.shape[1]]
        if tile >= 2:
            copy_out(tile - 2).wait()
        tile_ref[tile % 2] = block
        copy_out(tile).start()
    for tile in range(tiles - 2, tiles):
        copy_out(tile).wait()


SMEM = pl.BlockSpec(memory_space=pltpu.SMEM)
VMEM = pl.BlockSpec(memory_space=pltpu.VMEM)
ANY = pl.BlockSpec(memory_space=pl.ANY)
LIMIT = pltpu.CompilerParams(vmem_limit_bytes=16 * 2**20)


def body(passages, centroids, dual_init):
    depth = passages.shape[1]
    local_rows = passages.shape[0]
    count = centroids.shape[0]
    factor = 4.0 / math.sqrt(depth)
    devices = lax.axis_size(EVERY)
    z, h, x, _, c = coords(lax.axis_index(EVERY))
    first = jnp.where(c == 0, x, z)
    second = jnp.where(c == 0, z, x)

    def fetch(step):
        def target(z, h, x, l, c):
            stays = h == c
            if stays and step == 0:
                return None
            h, l, c = (h, l, c) if stays else (1 - h, 1 - l, 1 - c)
            return (z, h, x - step, l, c) if c == 0 else (z - step, h, x, l, c)

        return move(passages, target)

    mine = jnp.where(h == c, passages, fetch(0))
    top = jnp.concatenate([mine, fetch(1)], axis=0)
    bottom = jnp.concatenate([fetch(2), fetch(3)], axis=0)
    bottom, near_duals = lax.optimization_barrier((bottom, to_sibling(dual_init)))
    top_before, bottom_after = along_second(top, 1), along_second(bottom, -1)
    bottom_before, top_after = along_second(bottom, 1), along_second(top, -1)
    top_across, bottom_across = along_second(top_before, 1), along_second(bottom_after, -1)
    first_pieces = [top, bottom, top_before, bottom_after]
    last_pieces = [top_after, bottom_before, top_across, bottom_across]
    order = [c * 4 + (second + k) % 4 for k in OWN]
    order += [(1 - c) * 4 + (first + k) % 4 for k in OWN]
    row, lane = jnp.where(h == 0, z, 4 + x), jnp.where(h == 0, x, z) * local_rows
    order += [row, lane] + [x * local_rows, z * local_rows]
    order += [(4 - x) % 4 * local_rows, (4 - z) % 4 * local_rows]
    order = jnp.stack(order).astype(jnp.int32)

    pairs, first_pieces = lax.optimization_barrier(
        ((dual_init, near_duals, centroids, to_sibling(centroids)), first_pieces)
    )
    early = early_logits(factor, pairs[:2], pairs[2:], first_pieces)
    last_pieces, early = lax.optimization_barrier((last_pieces, early))
    late = late_logits(factor, order, early[:2], early[2:4], last_pieces, early[6], early[7])
    logits = [early[4], late[0], to_sibling(early[5]), to_sibling(late[1])]
    parts, arrived = late[2], [late[3]]
    span = LANES
    f32 = jnp.float32
    parts = to_every(parts)
    pieces = arrived + [to_sibling(array) for array in arrived]

    sent = jax.ShapeDtypeStruct((devices, CHUNKS, span), jnp.bfloat16)
    block = pl.BlockSpec((devices, CHUNKS, span), lambda: (0, 0, 0))
    sums = pltpu.VMEM((CHUNKS, span), f32)
    kernel, passage_first, centroid_first, partial = pl.pallas_call(
        first_kernel,
        in_specs=[SMEM, VMEM] + [ANY] * len(logits),
        out_specs=[VMEM] * 3 + [block],
        out_shape=[
            jax.ShapeDtypeStruct((CHUNKS, count, span), f32),
            jax.ShapeDtypeStruct((CHUNKS, span), f32),
            jax.ShapeDtypeStruct((count, 1), f32),
            sent,
        ],
        scratch_shapes=[sums, pltpu.SemaphoreType.DMA((len(logits),))],
        compiler_params=LIMIT,
    )(order, parts, *logits)
    partial, *pieces = lax.optimization_barrier((partial, *pieces))
    partial = pl.pallas_call(
        middle_kernel,
        in_specs=[SMEM, VMEM, VMEM],
        out_specs=block,
        out_shape=sent,
        scratch_shapes=[sums],
        compiler_params=LIMIT,
    )(order, to_every(partial), kernel)
    new_centroids, own_duals, centroid_duals = pl.pallas_call(
        last_kernel,
        in_specs=[SMEM] + [VMEM] * 4 + [ANY] * len(pieces),
        out_specs=[ANY, VMEM, VMEM],
        out_shape=[
            jax.ShapeDtypeStruct((count, depth), jnp.bfloat16),
            jax.ShapeDtypeStruct((1, local_rows), f32),
            jax.ShapeDtypeStruct((count // LANES, LANES), f32),
        ],
        scratch_shapes=[
            pltpu.VMEM((count, CHUNKS * span), jnp.bfloat16),
            pltpu.VMEM((depth // WIDTH, CHUNKS * span, WIDTH), jnp.bfloat16),
            pltpu.VMEM((2, count, WIDTH), jnp.bfloat16),
            sums,
            pltpu.SemaphoreType.DMA((depth // WIDTH,)),
            pltpu.SemaphoreType.DMA((2,)),
        ],
        compiler_params=pltpu.CompilerParams(vmem_limit_bytes=24 * 2**20),
    )(order, to_every(partial), kernel, passage_first, centroid_first, *pieces)
    own_duals = own_duals.reshape(local_rows)
    return (new_centroids, own_duals, centroid_duals.reshape(count))


def solution(mesh):
    in_specs = (P("psg", None), P(("psg", "cen"), None), P(("psg", "cen")))
    out_specs = (P(("psg", "cen"), None), P("psg"), P(("psg", "cen")))
    return jax.shard_map(body, mesh=mesh, in_specs=in_specs, out_specs=out_specs, check_vma=False)
```
